256 devices in a mesh: grp: 16 (over x_hi, y, core), dev: 16 (over x_lo, z).
Axes of the slice: x: 4 (x_hi: 2, x_lo: 2; x = x_hi * 2 + x_lo), y: 4, z: 8, core: 2. Of those that a mesh axis runs over, the one named last changes fastest.
Arguments:
- series: bfloat16 [16384, 6, 1024], P(('grp', 'dev')), may hold values from -6 to 6
- taps: bfloat16 [16384, 64], P(('grp', 'dev')), may hold values from -0.75 to 0.75
- keep: int32 [16384, 6], P(('grp', 'dev')), may hold values from 0 to 1, as said below
- offsets: int32 [8], replicated, may hold values from 1 to 256, as said below
Outputs:
- corr: float32 [16384, 8, 128], P(('grp', 'dev'))
- stack: float32 [8, 128], replicated
The draws below stay inside these ranges and needn't reach their ends.
Inputs may be any that keep to these rules, and one draw needn't show every extreme that they name: keep[c, s] is 1 where segment s of channel c is free of passing trains and usable; trains cover runs of neighbouring channels. 8 distinct channel offsets; 256 is always among them.
All inputs are finite; a program needn't handle non-finite values.
Results may differ from the reference program's by a relative error of at most 0.0041.
Values may be sent and summed in bfloat16 or wider, within the bound.
A program may use at most 128 MiB of HBM per device.

```python
import jax
import jax.numpy as jnp
from jax import lax

CH_DEV = 64
SEG = 6
SAMP = 1024
BLK = 128
TAPS = 64
NLAG = 128
REACH = 256
NOFF = 8
CHANNELS = 16384


def draw_keep(key, part):
    train_key, span_key, drop_key = jax.random.split(key, 3)
    centre = jax.random.randint(train_key, (3, SEG), 0, CHANNELS)
    reach_half = jax.random.randint(span_key, (3, SEG), CHANNELS // 64 + 1, CHANNELS // 10 + 2)
    channel = jnp.arange(CHANNELS, dtype=jnp.int32)[:, None, None]
    distance = jnp.abs(channel - centre[None])
    distance = jnp.minimum(distance, CHANNELS - distance)
    covered = jnp.any(distance < reach_half[None], axis=1)
    dropped = jax.random.randint(drop_key, (CHANNELS, SEG), 0, 8) == 0
    return jnp.where(covered | dropped, 0, 1).astype(jnp.int32)


def draw_offsets(key, part):
    pick_key, order_key = jax.random.split(key)
    chosen = jax.random.permutation(pick_key, REACH - 1)[:NOFF - 1].astype(jnp.int32) + 1
    values = jnp.concatenate([chosen, jnp.full((1,), REACH, jnp.int32)])
    return jax.random.permutation(order_key, values)


def block_levels(key, extent, cuts, smallest, high):
    gain = 1.0
    for position, blocks in cuts:
        draws = jax.random.uniform(jax.random.fold_in(jax.random.fold_in(key, 6), position), (blocks,), jnp.float32, smallest / len(cuts), high / len(cuts))
        gain = gain * jnp.repeat(jnp.exp(draws), extent[position] // blocks).reshape((-1,) + (1,) * (len(extent) - 1 - position))
    return gain


def gaussian(key, shape, spread, most, cuts=(), kind=jnp.bfloat16):
    level = block_levels(key, shape, cuts, -0.22, 0.18) if cuts else 1.0
    entries = jax.random.normal(key, shape, jnp.float32) * spread * level
    return jnp.minimum(jnp.maximum(entries, -most), most).astype(kind)


def setup_inputs(seed: int = 0) -> dict:
    key_of = jax.random.split(jax.random.key(seed), 5)
    series = gaussian(key_of[0], (CHANNELS, SEG, SAMP), 1.0, 6.0, ((0, 256),))
    taps = gaussian(key_of[1], (CHANNELS, TAPS), TAPS ** -0.5, 0.75, ((0, 256),))
    keep = draw_keep(jax.random.fold_in(key_of[4], 71), 0)
    offsets = draw_offsets(jax.random.fold_in(key_of[4], 71), 0)
    return {"series": series, "taps": taps, "keep": keep, "offsets": offsets}


def toeplitz_rows(taps_part, block_len):
    row_total = taps_part.shape[0]
    tap_count = taps_part.shape[1]
    lead_zeros = jnp.zeros((row_total, block_len - tap_count + 1), taps_part.dtype)
    trail_zeros = jnp.zeros((row_total, block_len), taps_part.dtype)
    pattern = jnp.concatenate([lead_zeros, taps_part[:, ::-1], trail_zeros], axis=1)
    repeated = jnp.tile(pattern, (1, block_len))
    return repeated[:, :block_len * 2 * block_len].reshape(row_total, block_len, 2 * block_len)

def whiten_group(series_part, taps_part):
    row_total, segment_count, sample_count = series_part.shape
    blocks = series_part.reshape(row_total, segment_count, sample_count // BLK, BLK)
    earlier = jnp.concatenate([jnp.zeros_like(blocks[:, :, :1]), blocks[:, :, :-1]], axis=2)
    windows = jnp.concatenate([earlier, blocks], axis=3)
    matrix = toeplitz_rows(taps_part, BLK)
    filtered = jnp.einsum('csbi,cji->csbj', windows.astype(jnp.float32), matrix.astype(jnp.float32), precision=lax.Precision.HIGHEST)
    return filtered.reshape(row_total, segment_count, sample_count).astype(jnp.bfloat16)

def reference(series, taps, keep, offsets):
    groups = CHANNELS // CH_DEV
    whitened = lax.map(lambda pair: whiten_group(pair[0], pair[1]), (series.reshape(groups, CH_DEV, SEG, SAMP), taps.reshape(groups, CH_DEV, TAPS)))
    whitened = whitened.reshape(CHANNELS, SEG, SAMP)
    length = SAMP + NLAG
    half_lag = NLAG // 2
    keep_float = keep.astype(jnp.float32)
    partner_index = (jnp.arange(CHANNELS, dtype=jnp.int32)[:, None] + offsets[None, :]) % CHANNELS
    paired = keep_float[:, None, :] * keep_float[partner_index]
    pair_count = lax.optimization_barrier(jnp.sum(paired, axis=2))
    weighted_sum = jnp.zeros((CHANNELS, NOFF, NLAG), jnp.float32)
    for segment in range(SEG):
        spectra = jnp.fft.rfft(whitened[:, segment].astype(jnp.float32), n=length, axis=1)

        def one_offset(offset_value):
            partner = jnp.roll(spectra, -offset_value, axis=0)
            circular = jnp.fft.irfft(jnp.conj(spectra) * partner, n=length, axis=1)
            return jnp.concatenate([circular[:, length - half_lag:], circular[:, :half_lag]], axis=1)
        lagged = lax.map(one_offset, offsets)
        weighted_sum = weighted_sum + paired[:, :, segment][:, :, None] * jnp.transpose(lagged, (1, 0, 2))
    divisor = jnp.maximum(pair_count, 1.0)[:, :, None] * jnp.sqrt(jnp.float32(SAMP))
    corr = weighted_sum / divisor
    stack = lax.optimization_barrier(jnp.sum(corr, axis=0)) / jnp.sqrt(jnp.float32(CHANNELS))
    return (corr, stack)
```

```python
import functools
import math

import jax
import jax.numpy as jnp
import numpy as np
from jax import lax
from jax.experimental import pallas as pl
from jax.experimental.pallas import tpu as pltpu
from jax.sharding import PartitionSpec as P

SEG = 6
SAMP = 1024
BLK = 128
NLAG = 128
NOFF = 8
CH = 64
NB = SAMP // BLK
NEAR = 3 * CH
GRP_CH = 16
MESH = pl.DeviceIdType.MESH


def dft_tables():
    n = np.arange(2 * BLK, dtype=np.float64)[:, None]
    f = np.arange(BLK, dtype=np.float64)[None, :] + 0.5
    ang = 2.0 * np.pi * f * n / (2 * BLK)
    full = np.concatenate([np.cos(ang), -np.sin(ang)], axis=1)
    half = BLK // 2
    own = full[:BLK]
    win = np.concatenate([full[half : half + BLK], full[half + BLK :], full[:half]], axis=0)

    def split(t):
        t32 = t.astype(np.float32)
        hi = t32.astype(jnp.bfloat16)
        lo = (t32 - hi.astype(np.float32)).astype(jnp.bfloat16)
        return hi, lo

    own_hi, own_lo = split(own)
    win_hi, win_lo = split(win)
    m = np.arange(NLAG, dtype=np.float64)[None, :]
    ang_inv = 2.0 * np.pi * f.T * m / (2 * BLK)
    inv = np.concatenate([np.cos(ang_inv), -np.sin(ang_inv)], axis=0) / BLK
    return (
        np.concatenate([own_hi, own_lo], axis=0),
        win_hi,
        win_lo,
        inv.astype(np.float32),
    )


def kernel(
    shape,
    ser,
    taps,
    keepv,
    keeps,
    offs,
    offv,
    t_own,
    t_hi,
    t_lo,
    t_inv,
    out,
    part,
    white,
    p1,
    p2,
    m2,
    k1,
    k2,
    km2,
    scr,
    keep_left,
    keep_near,
    xs,
    ys,
    accr,
    acci,
    cnt,
    res,
    res_send,
    res_recv,
    ssem,
    rsem,
):
    ng, nd = shape

    def dev(k):
        t = lax.axis_index("grp") * nd + lax.axis_index("dev") + (k + ng * nd)
        t = lax.rem(t, ng * nd)
        return (t // nd, lax.rem(t, nd))

    bar = pltpu.get_barrier_semaphore()
    for k in (-2, -1, 1, 2):
        pl.semaphore_signal(bar, inc=1, device_id=dev(k), device_id_type=MESH)

    for s in range(SEG):
        scr[pl.ds(s * 9 * GRP_CH, GRP_CH), :] = jnp.zeros((GRP_CH, BLK), jnp.float32)
    ri = lax.broadcasted_iota(jnp.int32, (BLK, BLK), 0)
    ci = lax.broadcasted_iota(jnp.int32, (BLK, BLK), 1)
    causal = ci >= ri

    @pl.loop(0, CH // GRP_CH)
    def _(g):
        for s in range(SEG):
            x = ser[s, pl.ds(g * GRP_CH, GRP_CH), :].astype(jnp.float32)
            for b in range(NB):
                scr[pl.ds((s * 9 + b + 1) * GRP_CH, GRP_CH), :] = x[:, b * BLK : (b + 1) * BLK]

        @pl.loop(0, GRP_CH // 2)
        def _(h):
            rows = []
            for e in range(2):
                c = h * 2 + e
                cur = [scr[pl.ds((s * 9 + 1) * GRP_CH + c, NB, stride=GRP_CH), :] for s in range(SEG)]
                prv = [scr[pl.ds(s * 9 * GRP_CH + c, NB, stride=GRP_CH), :] for s in range(SEG)]
                x = jnp.concatenate(
                    [jnp.concatenate(prv, axis=0), jnp.concatenate(cur, axis=0)], axis=1
                ).astype(jnp.bfloat16)
                row = taps[pl.ds(g * GRP_CH + c, 1), :]
                circ = pltpu.roll(jnp.broadcast_to(row, (BLK, BLK)), 0, 1, stride=1, stride_axis=0)
                toep = jnp.concatenate(
                    [jnp.where(causal, 0.0, circ), jnp.where(causal, circ, 0.0)], axis=0
                ).astype(jnp.bfloat16)
                rows.append(jnp.dot(x, toep, preferred_element_type=jnp.float32))
            for s in range(SEG):
                both = []
                for e in range(2):
                    flag = keeps[s, g * GRP_CH + h * 2 + e].astype(jnp.float32)
                    both.append(rows[e][s * NB : (s + 1) * NB] * flag)
                at = pl.multiple_of((g * GRP_CH + h * 2) * NB, 2 * NB)
                white[s, pl.ds(at, 2 * NB), :] = jnp.concatenate(both, axis=0).astype(jnp.bfloat16)

    pl.semaphore_wait(bar, 4)

    def remote(src, dst, lane, at, to):
        return pltpu.make_async_remote_copy(
            src_ref=src,
            dst_ref=dst,
            send_sem=ssem.at[lane, at],
            recv_sem=rsem.at[lane, at],
            device_id=dev(to),
            device_id_type=MESH,
        )

    def keep_copy(lane):
        if lane == 0:
            return remote(keepv, k1, 0, SEG, -1)
        if lane == 1:
            return remote(k1, k2, 1, SEG, -1)
        return remote(keepv, km2, 2, SEG, 2)

    def seg_copy(lane, s):
        if lane == 0:
            return remote(white.at[s], p1.at[s], 0, s, -1)
        if lane == 1:
            return remote(p1.at[s], p2.at[s], 1, s, -1)
        return remote(white.at[s], m2.at[s], 2, s, 2)

    keep_copy(0).start()
    keep_copy(2).start()

    @pl.loop(0, SEG)
    def _(s):
        seg_copy(0, s).start()
        seg_copy(2, s).start()

    keep_copy(0).wait_recv()
    keep_copy(1).start()

    zero = jnp.zeros((64, BLK), jnp.float32)

    @pl.loop(0, CH * NOFF * 8 // 64)
    def _(i):
        accr[pl.ds(i * 64, 64), :] = zero
        acci[pl.ds(i * 64, 64), :] = zero

    keep_left[pl.ds(0, CH), :] = keepv[...].astype(jnp.float32)
    keep_near[pl.ds(0, CH), :] = keepv[...].astype(jnp.float32)
    keep_near[pl.ds(CH, CH), :] = k1[...].astype(jnp.float32)

    def pair_rows(r, j):
        row = r + offs[j]
        home = row < NEAR
        return jnp.where(home, r, CH + r), jnp.where(home, row, row - 2 * CH)

    lane_i = lax.broadcasted_iota(jnp.int32, (16, NB, BLK), 2)
    blk_i = lax.broadcasted_iota(jnp.int32, (16, NB, BLK), 1)
    low = lane_i < BLK // 2
    first = blk_i == 0
    last = blk_i == NB - 1

    def window_dft(src, s, base):
        @pl.loop(0, CH // 16)
        def _(i):
            w = src[s, pl.ds(i * 128, 128), :]
            wf = w.astype(jnp.float32).reshape(16, NB, BLK)
            nxt = jnp.where(last, 0.0, pltpu.roll(wf, NB - 1, 1))
            prv = jnp.where(first, 0.0, pltpu.roll(wf, 1, 1))
            mix = jnp.where(low, nxt, prv).reshape(128, BLK).astype(jnp.bfloat16)
            x = jnp.concatenate([w, mix], axis=1)
            y = jnp.dot(x, t_hi[...], preferred_element_type=jnp.float32)
            y = y + jnp.dot(x, t_lo[...], preferred_element_type=jnp.float32)
            ys[pl.ds(base + i * 16, 16), :, :] = y.reshape(16, NB, 2 * BLK)

    def own_dft(src, s, base):
        @pl.loop(0, CH // 16)
        def _(i):
            w = src[s, pl.ds(i * 128, 128), :]
            x = jnp.concatenate([w, w], axis=1)
            y = jnp.dot(x, t_own[...], preferred_element_type=jnp.float32)
            xs[pl.ds(base + i * 16, 16), :, :] = y.reshape(16, NB, 2 * BLK)

    @pl.loop(0, SEG)
    def _(s):
        own_dft(white, s, 0)
        window_dft(white, s, 0)
        seg_copy(0, s).wait_recv()
        seg_copy(1, s).start()
        window_dft(p1, s, CH)
        seg_copy(2, s).wait_recv()
        own_dft(m2, s, CH)
        seg_copy(1, s).wait_recv()
        window_dft(p2, s, 2 * CH)

        @pl.loop(0, CH)
        def _(r):
            for j in range(NOFF):
                left, near = pair_rows(r, j)
                a = xs[left]
                b = ys[near]
                at = pl.ds(pl.multiple_of((r * NOFF + j) * 8, 8), 8)
                ar, ai = a[:, :BLK], a[:, BLK:]
                br, bi = b[:, :BLK], b[:, BLK:]
                accr[at, :] += ar * br + ai * bi
                acci[at, :] += ar * bi - ai * br

    keep_copy(1).wait_recv()
    keep_copy(2).wait_recv()
    keep_near[pl.ds(2 * CH, CH), :] = k2[...].astype(jnp.float32)
    keep_left[pl.ds(CH, CH), :] = km2[...].astype(jnp.float32)

    @pl.loop(0, CH)
    def _(r):
        prod = []
        for j in range(NOFF):
            left, near = pair_rows(r, j)
            prod.append(keep_left[pl.ds(left, 1), :] * keep_near[pl.ds(near, 1), :])
        at = pl.ds(pl.multiple_of(r * NOFF, NOFF), NOFF)
        cnt[at, :] = jnp.concatenate(prod, axis=0)

    ones = jnp.ones((BLK, BLK), jnp.bfloat16)
    part[...] = jnp.zeros((NOFF, NLAG), jnp.float32)

    def back_copy(q):
        rows = pl.ds(q * 128, 128)
        return remote(res_send.at[rows], res_recv.at[rows], 3, q, -2)

    for q in range(4):
        base = q * 128
        sr = jnp.zeros((128, BLK), jnp.float32)
        si = jnp.zeros((128, BLK), jnp.float32)
        for k in range(8):
            sr = sr + accr[pl.ds(base * 8 + k, 128, stride=8), :]
            si = si + acci[pl.ds(base * 8 + k, 128, stride=8), :]
        spec = jnp.concatenate([sr, si], axis=1)
        lag = jnp.dot(
            spec, t_inv[...], precision=lax.Precision.HIGHEST, preferred_element_type=jnp.float32
        )
        number = jnp.dot(
            cnt[pl.ds(base, 128), :].astype(jnp.bfloat16), ones, preferred_element_type=jnp.float32
        )
        corr = lag / (jnp.maximum(number, 1.0) * math.sqrt(SAMP))
        res[pl.ds(base, 128), :] = corr
        res_send[pl.ds(base, 128), :] = corr.astype(res_send.dtype)
        back_copy(q).start()
        part[...] += jnp.sum(corr.reshape(16, NOFF, NLAG), axis=0)

    for q in range(4):
        back_copy(q).wait_recv()
        for i in range(16):
            r = q * 16 + i
            home = offv[...] + r < NEAR
            got = res_recv[pl.ds(q * 128, 128), :].astype(jnp.float32)[i * 8 : (i + 1) * 8]
            out[r] = jnp.where(home, res[pl.ds(r * 8, 8), :], got)

    for q in range(4):
        back_copy(q).wait_send()

    @pl.loop(0, SEG)
    def _(s):
        for lane in range(3):
            seg_copy(lane, s).wait_send()

    for lane in range(3):
        keep_copy(lane).wait_send()


def local(shape, series, taps, keep, offsets):
    t_own, t_hi, t_lo, t_inv = dft_tables()
    ser = jnp.transpose(series, (1, 0, 2))
    taps_row = jnp.pad(taps.astype(jnp.float32), ((0, 0), (0, BLK - taps.shape[1])))
    keepv = jnp.pad(keep.astype(jnp.bfloat16), ((0, 0), (0, BLK - SEG)))
    keeps = jnp.transpose(keep, (1, 0))
    offv = jnp.broadcast_to(offsets[:, None], (NOFF, NLAG))
    vmem = pl.BlockSpec(memory_space=pltpu.VMEM)
    smem = pl.BlockSpec(memory_space=pltpu.SMEM)
    f32, b16 = jnp.float32, jnp.bfloat16
    rows = CH * NB
    corr, part = pl.pallas_call(
        functools.partial(kernel, shape),
        out_shape=(
            jax.ShapeDtypeStruct((CH, NOFF, NLAG), f32),
            jax.ShapeDtypeStruct((NOFF, NLAG), f32),
        ),
        in_specs=[vmem, vmem, vmem, smem, smem, vmem, vmem, vmem, vmem, vmem],
        out_specs=(vmem, vmem),
        scratch_shapes=[
            pltpu.VMEM((SEG, rows, BLK), b16),
            pltpu.VMEM((SEG, rows, BLK), b16),
            pltpu.VMEM((SEG, rows, BLK), b16),
            pltpu.VMEM((SEG, rows, BLK), b16),
            pltpu.VMEM((CH, BLK), b16),
            pltpu.VMEM((CH, BLK), b16),
            pltpu.VMEM((CH, BLK), b16),
            pltpu.VMEM((SEG * 9 * GRP_CH, BLK), f32),
            pltpu.VMEM((2 * CH, BLK), f32),
            pltpu.VMEM((NEAR, BLK), f32),
            pltpu.VMEM((2 * CH, NB, 2 * BLK), f32),
            pltpu.VMEM((NEAR, NB, 2 * BLK), f32),
            pltpu.VMEM((CH * NOFF * 8, BLK), f32),
            pltpu.VMEM((CH * NOFF * 8, BLK), f32),
            pltpu.VMEM((CH * NOFF, BLK), f32),
            pltpu.VMEM((CH * NOFF, BLK), f32),
            pltpu.VMEM((CH * NOFF, BLK), b16),
            pltpu.VMEM((CH * NOFF, BLK), b16),
            pltpu.SemaphoreType.DMA((4, SEG + 1)),
            pltpu.SemaphoreType.DMA((4, SEG + 1)),
        ],
        compiler_params=pltpu.CompilerParams(
            collective_id=0, has_side_effects=True, vmem_limit_bytes=40 << 20
        ),
        name="whiten_correlate",
    )(ser, taps_row, keepv, keeps, offsets, offv, t_own, t_hi, t_lo, t_inv)
    stack = lax.psum(part, ("grp", "dev")) / math.sqrt(CH * shape[0] * shape[1])
    return corr, stack


def solution(mesh):
    spec3 = P(("grp", "dev"), None, None)
    spec2 = P(("grp", "dev"), None)
    shape = (mesh.shape["grp"], mesh.shape["dev"])
    return jax.shard_map(
        functools.partial(local, shape),
        mesh=mesh,
        in_specs=(spec3, spec2, spec2, P()),
        out_specs=(spec3, P()),
        check_vma=False,
    )
```

```python
import functools
import math

import jax
import jax.numpy as jnp
import numpy as np
from jax import lax
from jax.experimental import pallas as pl
from jax.experimental.pallas import tpu as pltpu
from jax.sharding import PartitionSpec as P

SEG = 6
SAMP = 1024
BLK = 128
TAPS = 64
NLAG = 128
NOFF = 8
CH = 64
NB = SAMP // BLK
NEAR = 3 * CH
EXT = 5 * CH
GRP_CH = 16
ROWS = NB * CH
PAD_ROWS = ROWS + 2 * CH
QUART = 4
MESH = pl.DeviceIdType.MESH


def dft_tables():
    n = np.arange(2 * BLK, dtype=np.float64)[:, None]
    f = np.arange(BLK, dtype=np.float64)[None, :] + 0.5
    ang = 2.0 * np.pi * f * n / (2 * BLK)
    full = np.concatenate([np.cos(ang), -np.sin(ang)], axis=1)
    half = BLK // 2
    own = full[:BLK]
    win = np.concatenate([full[half : half + BLK], full[half + BLK :], full[:half]], axis=0)

    def split(t):
        t32 = t.astype(np.float32)
        hi = t32.astype(jnp.bfloat16)
        lo = (t32 - hi.astype(np.float32)).astype(jnp.bfloat16)
        return hi, lo

    own_hi, own_lo = split(own)
    win_hi, win_lo = split(win)
    m = np.arange(NLAG, dtype=np.float64)[None, :]
    ang_inv = 2.0 * np.pi * f.T * m / (2 * BLK)
    inv = np.concatenate([np.cos(ang_inv), -np.sin(ang_inv)], axis=0) / BLK
    return (
        np.concatenate([own_hi, own_lo], axis=0),
        np.concatenate([win_hi, win_lo], axis=0),
        inv.astype(np.float32),
    )


def kernel(
    shape,
    ser_hbm,
    tk,
    offs,
    own_hbm,
    win_hbm,
    inv_hbm,
    out,
    stack,
    ser,
    t_own,
    t_win,
    t_inv,
    white,
    p1,
    p2,
    m2,
    kv,
    k1,
    k2,
    km2,
    scr,
    keep_near,
    keep_left,
    xr,
    xi,
    yr,
    yi,
    accr,
    acci,
    cnt,
    res,
    res_send,
    res_recv,
    part,
    got_a,
    got_b,
    ssem,
    rsem,
    asem,
    bsem,
    lsem,
):
    ng, nd = shape
    f32, b16 = jnp.float32, jnp.bfloat16
    me_g, me_d = lax.axis_index("grp"), lax.axis_index("dev")

    def dev(k):
        t = lax.rem(me_g * nd + me_d + (k + ng * nd), ng * nd)
        return (t // nd, lax.rem(t, nd))

    def along_dev(k):
        return (me_g, lax.rem(me_d + k, nd))

    def along_grp(k):
        return (lax.rem(me_g + k, ng), me_d)

    loads = [
        pltpu.make_async_copy(
            ser_hbm.at[:, pl.ds(g * GRP_CH, GRP_CH), :],
            ser.at[:, pl.ds(g * GRP_CH, GRP_CH), :],
            lsem.at[g],
        )
        for g in range(CH // GRP_CH)
    ]
    loads += [
        pltpu.make_async_copy(own_hbm, t_own, lsem.at[4]),
        pltpu.make_async_copy(win_hbm, t_win, lsem.at[5]),
        pltpu.make_async_copy(inv_hbm, t_inv, lsem.at[6]),
    ]
    for copy in loads:
        copy.start()

    bar = pltpu.get_barrier_semaphore()
    for k in (-2, -1, 1, 2):
        pl.semaphore_signal(bar, inc=1, device_id=dev(k), device_id_type=MESH)
    for k in range(1, nd):
        pl.semaphore_signal(bar, inc=1, device_id=along_dev(k), device_id_type=MESH)
    for k in range(1, ng):
        pl.semaphore_signal(bar, inc=1, device_id=along_grp(k), device_id_type=MESH)

    for s in range(SEG):
        scr[pl.ds(s * 9 * GRP_CH, GRP_CH), :] = jnp.zeros((GRP_CH, BLK), f32)
        for ref in (white, p1, p2):
            ref[s, pl.ds(0, CH), :] = jnp.zeros((CH, BLK), b16)
            ref[s, pl.ds(ROWS + CH, CH), :] = jnp.zeros((CH, BLK), b16)
    accr[...] = jnp.zeros_like(accr)
    acci[...] = jnp.zeros_like(acci)

    lane = lax.broadcasted_iota(jnp.int32, (CH, BLK), 1)
    kv[...] = jnp.where(lane < TAPS, 0.0, tk[...]).astype(b16)

    row_i = lax.broadcasted_iota(jnp.int32, (BLK, BLK), 0)
    col_i = lax.broadcasted_iota(jnp.int32, (BLK, BLK), 1)
    causal = col_i >= row_i
    row_lane = lax.broadcasted_iota(jnp.int32, (1, BLK), 1)

    for g in range(CH // GRP_CH):
        loads[g].wait()
        for s in range(SEG):
            for b in range(NB):
                x = ser[s, pl.ds(g * GRP_CH, GRP_CH), pl.ds(b * BLK, BLK)]
                scr[pl.ds((s * 9 + b + 1) * GRP_CH, GRP_CH), :] = x.astype(f32)

        @pl.loop(0, GRP_CH, unroll=2)
        def _(c):
            cur = [scr[pl.ds((s * 9 + 1) * GRP_CH + c, NB, stride=GRP_CH), :] for s in range(SEG)]
            prv = [scr[pl.ds(s * 9 * GRP_CH + c, NB, stride=GRP_CH), :] for s in range(SEG)]
            x = jnp.concatenate(
                [jnp.concatenate(prv, axis=0), jnp.concatenate(cur, axis=0)], axis=1
            ).astype(b16)
            row = jnp.where(row_lane < TAPS, tk[pl.ds(g * GRP_CH + c, 1), :], 0.0)
            circ = pltpu.roll(jnp.broadcast_to(row, (BLK, BLK)), 0, 1, stride=1, stride_axis=0)
            toep = jnp.concatenate(
                [jnp.where(causal, 0.0, circ), jnp.where(causal, circ, 0.0)], axis=0
            ).astype(b16)
            y = jnp.dot(x, toep, preferred_element_type=f32)
            for s in range(SEG):
                scr[pl.ds((s * 9 + 1) * GRP_CH + c, NB, stride=GRP_CH), :] = y[s * NB : (s + 1) * NB]

        flags = tk[pl.ds(g * GRP_CH, GRP_CH), :]
        for s in range(SEG):
            flag = jnp.broadcast_to(flags[:, TAPS + s : TAPS + s + 1], (GRP_CH, BLK))
            for b in range(NB):
                y = scr[pl.ds((s * 9 + b + 1) * GRP_CH, GRP_CH), :] * flag
                white[s, pl.ds((b + 1) * CH + g * GRP_CH, GRP_CH), :] = y.astype(b16)

    def remote(src, dst, line, at, to):
        return pltpu.make_async_remote_copy(
            src_ref=src,
            dst_ref=dst,
            send_sem=ssem.at[line, at],
            recv_sem=rsem.at[line, at],
            device_id=dev(to),
            device_id_type=MESH,
        )

    def keep_copy(line):
        if line == 0:
            return remote(kv, k1, 0, SEG, -1)
        if line == 1:
            return remote(k1, k2, 1, SEG, -1)
        return remote(kv, km2, 2, SEG, 2)

    def seg_copy(line, s):
        body = pl.ds(CH, ROWS)
        if line == 0:
            return remote(white.at[s, body], p1.at[s, body], 0, s, -1)
        if line == 1:
            return remote(p1.at[s, body], p2.at[s, body], 1, s, -1)
        return remote(white.at[s, body], m2.at[s], 2, s, 2)

    def window_dft(src, s, bases):
        nxt = jnp.where(row_lane < BLK // 2, 1.0, 0.0).astype(b16)
        prv = jnp.where(row_lane < BLK // 2, 0.0, 1.0).astype(b16)
        cur = src[s, pl.ds(CH, ROWS), :]
        mix = src[s, pl.ds(2 * CH, ROWS), :] * nxt + src[s, pl.ds(0, ROWS), :] * prv
        x = jnp.concatenate([cur, mix, cur, mix], axis=1)
        y = jnp.dot(x, t_win[...], preferred_element_type=f32)
        for b in range(NB):
            for base in bases:
                yr[pl.ds(b * EXT + base, CH), :] = y[b * CH : (b + 1) * CH, :BLK]
                yi[pl.ds(b * EXT + base, CH), :] = y[b * CH : (b + 1) * CH, BLK:]

    def own_dft(src, s, start, base):
        w = src[s, pl.ds(start, ROWS), :]
        y = jnp.dot(jnp.concatenate([w, w], axis=1), t_own[...], preferred_element_type=f32)
        for b in range(NB):
            xr[pl.ds(b * 2 * CH + base, CH), :] = y[b * CH : (b + 1) * CH, :BLK]
            xi[pl.ds(b * 2 * CH + base, CH), :] = y[b * CH : (b + 1) * CH, BLK:]

    eight = lax.broadcasted_iota(jnp.int32, (8, BLK), 0)

    def away(j, r0):
        return eight + (r0 + offs[j]) >= NEAR

    def pairs(g):
        r0 = pl.multiple_of(g * 8, 8)
        far = [away(j, r0) for j in range(NOFF)]
        tr = [accr[pl.ds(j * CH + r0, 8), :] for j in range(NOFF)]
        ti = [acci[pl.ds(j * CH + r0, 8), :] for j in range(NOFF)]
        for b in range(NB):
            ar = xr[pl.ds(b * 2 * CH + r0, 8), :]
            ai = xi[pl.ds(b * 2 * CH + r0, 8), :]
            cr = xr[pl.ds(b * 2 * CH + CH + r0, 8), :]
            ci = xi[pl.ds(b * 2 * CH + CH + r0, 8), :]
            for j in range(NOFF):
                near = pl.ds(b * EXT + r0 + offs[j], 8)
                br = yr[near, :]
                bi = yi[near, :]
                lr = jnp.where(far[j], cr, ar)
                li = jnp.where(far[j], ci, ai)
                tr[j] = tr[j] + (lr * br + li * bi)
                ti[j] = ti[j] + (lr * bi - li * br)
        for j in range(NOFF):
            accr[pl.ds(j * CH + r0, 8), :] = tr[j]
            acci[pl.ds(j * CH + r0, 8), :] = ti[j]

    def first_dfts(s):
        own_dft(white, s, CH, 0)
        window_dft(white, s, (0,))
        window_dft(p1, s, (CH, 3 * CH))

    def last_dfts(s):
        own_dft(m2, s, 0, CH)
        window_dft(p2, s, (2 * CH, 4 * CH))

    pl.semaphore_wait(bar, 4 + (nd - 1) + (ng - 1))
    keep_copy(0).start()
    keep_copy(2).start()
    seg_copy(0, 0).start()
    seg_copy(0, 1).start()
    for s in range(SEG):
        seg_copy(2, s).start()
    keep_copy(0).wait_recv()
    keep_copy(1).start()
    for copy in loads[4:]:
        copy.wait()

    @pl.loop(0, SEG)
    def _(s):
        seg_copy(0, s).wait_recv()
        seg_copy(1, s).start()

        @pl.when(s < SEG - 2)
        def _():
            seg_copy(0, s + 2).start()

        @pl.when(s > 0)
        def _():
            seg_copy(1, s - 1).wait_recv()
            seg_copy(2, s - 1).wait_recv()
            last_dfts(s - 1)

            @pl.loop(0, CH // 8)
            def _(g):
                pairs(g)

        first_dfts(s)

    keep_copy(1).wait_recv()
    keep_copy(2).wait_recv()
    keep_left[pl.ds(0, CH), :] = kv[...].astype(f32)
    keep_left[pl.ds(CH, CH), :] = km2[...].astype(f32)
    keep_near[pl.ds(0, CH), :] = kv[...].astype(f32)
    for base in (CH, 3 * CH):
        keep_near[pl.ds(base, CH), :] = k1[...].astype(f32)
    for base in (2 * CH, 4 * CH):
        keep_near[pl.ds(base, CH), :] = k2[...].astype(f32)

    @pl.loop(0, CH // 8)
    def _(g):
        r0 = pl.multiple_of(g * 8, 8)
        a = keep_left[pl.ds(r0, 8), :]
        c = keep_left[pl.ds(CH + r0, 8), :]
        for j in range(NOFF):
            near = keep_near[pl.ds(r0 + offs[j], 8), :]
            cnt[pl.ds(j * CH + r0, 8), :] = jnp.where(away(j, r0), c, a) * near

    ones = jnp.ones((BLK, BLK), b16)
    per = CH // QUART

    def back_copy(q):
        rows = pl.ds(q * per * NOFF, per * NOFF)
        return remote(res_send.at[rows], res_recv.at[rows], 3, q, -2)

    seg_copy(1, SEG - 1).wait_recv()
    seg_copy(2, SEG - 1).wait_recv()
    last_dfts(SEG - 1)

    part[...] = jnp.zeros((NOFF, NLAG), f32)
    for q in range(QUART):

        @pl.loop(q * per // 8, (q + 1) * per // 8)
        def _(g):
            pairs(g)

        rows = [pl.ds(j * CH + q * per, per) for j in range(NOFF)]
        spec = jnp.concatenate(
            [
                jnp.concatenate([accr[r, :] for r in rows], axis=0),
                jnp.concatenate([acci[r, :] for r in rows], axis=0),
            ],
            axis=1,
        )
        lag = jnp.dot(spec, t_inv[...], precision=lax.Precision.HIGHEST, preferred_element_type=f32)
        both = jnp.concatenate([cnt[r, :] for r in rows], axis=0).astype(b16)
        number = jnp.dot(both, ones, preferred_element_type=f32)
        corr = lag / (jnp.maximum(number, 1.0) * math.sqrt(SAMP))
        at = pl.ds(q * per * NOFF, per * NOFF)
        res[at, :] = corr
        res_send[at, :] = corr.astype(b16)
        back_copy(q).start()
        part[...] += jnp.concatenate(
            [jnp.sum(corr[j * per : (j + 1) * per], axis=0, keepdims=True) for j in range(NOFF)],
            axis=0,
        )

    def sum_copy(src, got, sem, k, to):
        return pltpu.make_async_remote_copy(
            src_ref=src,
            dst_ref=got.at[k],
            send_sem=sem.at[0, k],
            recv_sem=sem.at[1, k],
            device_id=to,
            device_id_type=MESH,
        )

    for k in range(1, nd):
        sum_copy(part, got_a, asem, k, along_dev(k)).start()
    got_a[0] = part[...]
    for k in range(1, nd):
        sum_copy(part, got_a, asem, k, along_dev(k)).wait_recv()
    got_b[0] = jnp.sum(got_a[...], axis=0)
    for k in range(1, ng):
        sum_copy(got_b.at[0], got_b, bsem, k, along_grp(k)).start()

    for q in range(QUART):
        back_copy(q).wait_recv()
        for j in range(NOFF):
            at = pl.ds((q * NOFF + j) * per, per)
            mine = res[at, :]
            theirs = res_recv[at, :].astype(f32)
            for h in range(per // 8):
                r0 = q * per + h * 8
                val = jnp.where(away(j, r0), theirs[h * 8 : h * 8 + 8], mine[h * 8 : h * 8 + 8])
                out[pl.ds(r0 * NOFF + j, 8, stride=NOFF), :] = val

    for k in range(1, ng):
        sum_copy(got_b.at[0], got_b, bsem, k, along_grp(k)).wait_recv()
    stack[...] = jnp.sum(got_b[...], axis=0) * (1.0 / math.sqrt(CH * nd * ng))

    for k in range(1, nd):
        sum_copy(part, got_a, asem, k, along_dev(k)).wait_send()
    for k in range(1, ng):
        sum_copy(got_b.at[0], got_b, bsem, k, along_grp(k)).wait_send()
    for q in range(QUART):
        back_copy(q).wait_send()

    @pl.loop(0, SEG)
    def _(s):
        for line in range(3):
            seg_copy(line, s).wait_send()

    for line in range(3):
        keep_copy(line).wait_send()


def local(shape, series, taps, keep, offsets):
    ng, nd = shape
    f32, b16 = jnp.float32, jnp.bfloat16
    ser = jnp.transpose(series, (1, 0, 2))
    tk = jnp.concatenate(
        [taps.astype(f32), keep.astype(f32), jnp.zeros((CH, BLK - TAPS - SEG), f32)], axis=1
    )
    vmem = pl.BlockSpec(memory_space=pltpu.VMEM)
    smem = pl.BlockSpec(memory_space=pltpu.SMEM)
    hbm = pl.BlockSpec(memory_space=pltpu.HBM)
    pairs = CH * NOFF
    vm = pltpu.VMEM
    corr, stack = pl.pallas_call(
        functools.partial(kernel, shape),
        out_shape=(
            jax.ShapeDtypeStruct((pairs, NLAG), f32),
            jax.ShapeDtypeStruct((NOFF, NLAG), f32),
        ),
        in_specs=[hbm, vmem, smem, hbm, hbm, hbm],
        out_specs=(vmem, vmem),
        scratch_shapes=[
            vm((SEG, CH, SAMP), b16),
            vm((2 * BLK, 2 * BLK), b16),
            vm((4 * BLK, 2 * BLK), b16),
            vm((2 * BLK, NLAG), f32),
            vm((SEG, PAD_ROWS, BLK), b16),
            vm((SEG, PAD_ROWS, BLK), b16),
            vm((SEG, PAD_ROWS, BLK), b16),
            vm((SEG, ROWS, BLK), b16),
            vm((CH, BLK), b16),
            vm((CH, BLK), b16),
            vm((CH, BLK), b16),
            vm((CH, BLK), b16),
            vm((SEG * 9 * GRP_CH, BLK), f32),
            vm((EXT, BLK), f32),
            vm((2 * CH, BLK), f32),
            vm((NB * 2 * CH, BLK), f32),
            vm((NB * 2 * CH, BLK), f32),
            vm((NB * EXT, BLK), f32),
            vm((NB * EXT, BLK), f32),
            vm((pairs, BLK), f32),
            vm((pairs, BLK), f32),
            vm((pairs, BLK), f32),
            vm((pairs, NLAG), f32),
            vm((pairs, NLAG), b16),
            vm((pairs, NLAG), b16),
            vm((NOFF, NLAG), f32),
            vm((nd, NOFF, NLAG), f32),
            vm((ng, NOFF, NLAG), f32),
            pltpu.SemaphoreType.DMA((4, SEG + 1)),
            pltpu.SemaphoreType.DMA((4, SEG + 1)),
            pltpu.SemaphoreType.DMA((2, nd)),
            pltpu.SemaphoreType.DMA((2, ng)),
            pltpu.SemaphoreType.DMA((7,)),
        ],
        compiler_params=pltpu.CompilerParams(
            collective_id=0, has_side_effects=True, vmem_limit_bytes=48 << 20
        ),
        name="whiten_correlate",
    )(ser, tk, offsets, *dft_tables())
    return corr.reshape(CH, NOFF, NLAG), stack


def solution(mesh):
    spec3 = P(("grp", "dev"), None, None)
    spec2 = P(("grp", "dev"), None)
    shape = (mesh.shape["grp"], mesh.shape["dev"])
    return jax.shard_map(
        functools.partial(local, shape),
        mesh=mesh,
        in_specs=(spec3, spec2, spec2, P()),
        out_specs=(spec3, P()),
        check_vma=False,
    )
```

```python
import functools
import math

import jax
import jax.numpy as jnp
import numpy as np
from jax import lax
from jax.experimental import pallas as pl
from jax.experimental.pallas import tpu as pltpu
from jax.sharding import PartitionSpec as P

SEG = 6
SAMP = 1024
BLK = 128
TAPS = 64
NLAG = 128
NOFF = 8
CH = 64
NB = SAMP // BLK
NEAR = 3 * CH
EXT = 5 * CH
GRP_CH = 16
ROWS = NB * CH
EARLY = 3
QUART = 4
MESH = pl.DeviceIdType.MESH


def split(t):
    t32 = t.astype(np.float32)
    hi = t32.astype(jnp.bfloat16)
    lo = (t32 - hi.astype(np.float32)).astype(jnp.bfloat16)
    return hi, lo


def dft_tables():
    n = np.arange(2 * BLK, dtype=np.float64)[:, None]
    f = np.arange(BLK, dtype=np.float64)[None, :] + 0.5
    ang = 2.0 * np.pi * f * n / (2 * BLK)
    full = np.concatenate([np.cos(ang), -np.sin(ang)], axis=1)
    half = BLK // 2
    own = full[:BLK]
    win = np.concatenate([full[half : half + BLK], full[half + BLK :], full[:half]], axis=0)
    m = np.arange(NLAG, dtype=np.float64)[None, :]
    ang_inv = 2.0 * np.pi * f.T * m / (2 * BLK)
    inv_hi, inv_lo = split(np.concatenate([np.cos(ang_inv), -np.sin(ang_inv)], axis=0) / BLK)
    inv = np.concatenate(
        [
            np.concatenate([inv_hi, inv_lo], axis=1),
            np.concatenate([inv_hi, np.zeros_like(inv_lo)], axis=1),
        ],
        axis=0,
    )
    return np.concatenate(split(own), axis=0), np.concatenate(split(win), axis=0), inv


def kernel(
    shape,
    ser_hbm,
    taps_hbm,
    keep_hbm,
    offs,
    own_hbm,
    win_hbm,
    inv_hbm,
    out,
    stack,
    ser,
    taps_in,
    keep_in,
    t_own,
    t_win,
    t_inv,
    white,
    p1,
    p2,
    m2,
    kv,
    k1,
    k2,
    km2,
    kt,
    tk,
    scr,
    keep_near,
    keep_left,
    xr,
    xi,
    yr,
    yi,
    accr,
    acci,
    scale,
    res,
    res_send,
    res_recv,
    part,
    got_a,
    got_b,
    ssem,
    rsem,
    asem,
    bsem,
    lsem,
):
    ng, nd = shape
    f32, b16 = jnp.float32, jnp.bfloat16
    me_g, me_d = lax.axis_index("grp"), lax.axis_index("dev")

    def dev(k):
        t = lax.rem(me_g * nd + me_d + (k + ng * nd), ng * nd)
        return (t // nd, lax.rem(t, nd))

    def along_dev(k):
        return (me_g, lax.rem(me_d + k, nd))

    def along_grp(k):
        return (lax.rem(me_g + k, ng), me_d)

    bar = pltpu.get_barrier_semaphore()
    for k in (-2, -1, 1, 2):
        pl.semaphore_signal(bar, inc=1, device_id=dev(k), device_id_type=MESH)

    groups = CH // GRP_CH
    small = [
        pltpu.make_async_copy(taps_hbm, taps_in, lsem.at[groups]),
        pltpu.make_async_copy(keep_hbm, keep_in, lsem.at[groups + 1]),
    ]
    loads = [
        pltpu.make_async_copy(
            ser_hbm.at[:, pl.ds(g * GRP_CH, GRP_CH), :],
            ser.at[:, pl.ds(g * GRP_CH, GRP_CH), :],
            lsem.at[g],
        )
        for g in range(groups)
    ]
    tables = [
        pltpu.make_async_copy(src, dst, lsem.at[groups + 2 + i])
        for i, (src, dst) in enumerate(((own_hbm, t_own), (win_hbm, t_win), (inv_hbm, t_inv)))
    ]
    for copy in small + loads + tables:
        copy.start()

    for k in range(1, nd):
        pl.semaphore_signal(bar, inc=1, device_id=along_dev(k), device_id_type=MESH)
    for k in range(1, ng):
        pl.semaphore_signal(bar, inc=1, device_id=along_grp(k), device_id_type=MESH)

    kt[...] = jnp.zeros_like(kt)
    tk[...] = jnp.zeros_like(tk)
    for s in range(SEG):
        scr[pl.ds(s * 9 * GRP_CH, GRP_CH), :] = jnp.zeros((GRP_CH, BLK), f32)
    for copy in small:
        copy.wait()
    tk[:, pl.ds(0, TAPS)] = taps_in[...].astype(f32)
    kt[pl.ds(0, SEG), pl.ds(0, CH)] = keep_in[...].astype(f32)
    flags = jnp.transpose(kt[...])[:CH]
    keep_left[pl.ds(0, CH), :] = flags
    kv[...] = flags.astype(b16)

    def remote(src, dst, line, at, to):
        return pltpu.make_async_remote_copy(
            src_ref=src,
            dst_ref=dst,
            send_sem=ssem.at[line, at],
            recv_sem=rsem.at[line, at],
            device_id=dev(to),
            device_id_type=MESH,
        )

    def keep_copy(line):
        if line == 0:
            return remote(kv, k1, 0, SEG, -1)
        if line == 1:
            return remote(k1, k2, 1, SEG, -1)
        return remote(kv, km2, 2, SEG, 2)

    def seg_copy(line, s, first=0, count=CH):
        blocks, rows = pl.ds(1, NB), pl.ds(first, count)
        if line == 0:
            return remote(white.at[s, blocks, rows], p1.at[s, blocks, rows], 0, s, -1)
        if line == 1:
            return remote(p1.at[s, blocks, rows], p2.at[s, blocks, rows], 1, s, -1)
        return remote(white.at[s, blocks, rows], m2.at[s, :, rows], 2, s, 2)

    row_i = lax.broadcasted_iota(jnp.int32, (BLK, BLK), 0)
    col_i = lax.broadcasted_iota(jnp.int32, (BLK, BLK), 1)
    causal = col_i >= row_i
    row_lane = lax.broadcasted_iota(jnp.int32, (1, BLK), 1)

    for g in range(groups):
        loads[g].wait()
        for s in range(SEG):
            for b in range(NB):
                x = ser[s, pl.ds(g * GRP_CH, GRP_CH), pl.ds(b * BLK, BLK)]
                scr[pl.ds((s * 9 + b + 1) * GRP_CH, GRP_CH), :] = x.astype(f32)

        @pl.loop(0, GRP_CH, unroll=2)
        def _(c):
            cur = [scr[pl.ds((s * 9 + 1) * GRP_CH + c, NB, stride=GRP_CH), :] for s in range(SEG)]
            prv = [scr[pl.ds(s * 9 * GRP_CH + c, NB, stride=GRP_CH), :] for s in range(SEG)]
            x = jnp.concatenate(
                [jnp.concatenate(prv, axis=0), jnp.concatenate(cur, axis=0)], axis=1
            ).astype(b16)
            row = tk[pl.ds(g * GRP_CH + c, 1), :]
            circ = pltpu.roll(jnp.broadcast_to(row, (BLK, BLK)), 0, 1, stride=1, stride_axis=0)
            toep = jnp.concatenate(
                [jnp.where(causal, 0.0, circ), jnp.where(causal, circ, 0.0)], axis=0
            ).astype(b16)
            y = jnp.dot(x, toep, preferred_element_type=f32)
            for s in range(SEG):
                scr[pl.ds((s * 9 + 1) * GRP_CH + c, NB, stride=GRP_CH), :] = y[s * NB : (s + 1) * NB]

        mine = keep_left[pl.ds(g * GRP_CH, GRP_CH), :]
        for s in range(SEG):
            flag = jnp.broadcast_to(mine[:, s : s + 1], (GRP_CH, BLK))
            for b in range(NB):
                y = scr[pl.ds((s * 9 + b + 1) * GRP_CH, GRP_CH), :] * flag
                white[s, b + 1, pl.ds(g * GRP_CH, GRP_CH), :] = y.astype(b16)
        if g == 0:
            pl.semaphore_wait(bar, 4 + (nd - 1) + (ng - 1))
            keep_copy(0).start()
            keep_copy(2).start()
        for s in range(EARLY):
            seg_copy(0, s, g * GRP_CH, GRP_CH).start()
            seg_copy(2, s, g * GRP_CH, GRP_CH).start()

    for s in range(EARLY, SEG):
        seg_copy(2, s).start()
    keep_copy(0).wait_recv()
    keep_copy(1).start()

    for s in range(SEG):
        for ref in (white, p1, p2):
            ref[s, 0] = jnp.zeros((CH, BLK), b16)
            ref[s, NB + 1] = jnp.zeros((CH, BLK), b16)
    accr[...] = jnp.zeros_like(accr)
    acci[...] = jnp.zeros_like(acci)

    def window_dft(src, s, bases):
        nxt = jnp.where(row_lane < BLK // 2, 1.0, 0.0).astype(b16)
        prv = jnp.where(row_lane < BLK // 2, 0.0, 1.0).astype(b16)
        cur = src[s, pl.ds(1, NB)].reshape(ROWS, BLK)
        mix = src[s, pl.ds(2, NB)].reshape(ROWS, BLK) * nxt + src[s, pl.ds(0, NB)].reshape(ROWS, BLK) * prv
        x = jnp.concatenate([cur, mix, cur, mix], axis=1)
        y = jnp.dot(x, t_win[...], preferred_element_type=f32)
        for b in range(NB):
            for base in bases:
                yr[pl.ds(b * EXT + base, CH), :] = y[b * CH : (b + 1) * CH, :BLK]
                yi[pl.ds(b * EXT + base, CH), :] = y[b * CH : (b + 1) * CH, BLK:]

    def own_dft(src, s, start, base):
        w = src[s, pl.ds(start, NB)].reshape(ROWS, BLK)
        y = jnp.dot(jnp.concatenate([w, w], axis=1), t_own[...], preferred_element_type=f32)
        for b in range(NB):
            xr[pl.ds(b * 2 * CH + base, CH), :] = y[b * CH : (b + 1) * CH, :BLK]
            xi[pl.ds(b * 2 * CH + base, CH), :] = y[b * CH : (b + 1) * CH, BLK:]

    eight = lax.broadcasted_iota(jnp.int32, (8, BLK), 0)
    per = CH // QUART

    def away(j, r0):
        return eight + (r0 + offs[j]) >= NEAR

    def slot(g, j):
        first = (g // (per // 8)) * (per * NOFF) + lax.rem(g, per // 8) * 8
        return pl.ds(pl.multiple_of(first + j * per, 8), 8)

    def pair_sums(g):
        r0 = pl.multiple_of(g * 8, 8)
        far = [away(j, r0) for j in range(NOFF)]
        tr = [accr[slot(g, j), :] for j in range(NOFF)]
        ti = [acci[slot(g, j), :] for j in range(NOFF)]
        for b in range(NB):
            ar = xr[pl.ds(b * 2 * CH + r0, 8), :]
            ai = xi[pl.ds(b * 2 * CH + r0, 8), :]
            cr = xr[pl.ds(b * 2 * CH + CH + r0, 8), :]
            ci = xi[pl.ds(b * 2 * CH + CH + r0, 8), :]
            for j in range(NOFF):
                near = pl.ds(b * EXT + r0 + offs[j], 8)
                br = yr[near, :]
                bi = yi[near, :]
                lr = jnp.where(far[j], cr, ar)
                li = jnp.where(far[j], ci, ai)
                tr[j] = tr[j] + (lr * br + li * bi)
                ti[j] = ti[j] + (lr * bi - li * br)
        return tr, ti

    def first_dfts(s):
        own_dft(white, s, 1, 0)
        window_dft(white, s, (0,))
        window_dft(p1, s, (CH, 3 * CH))

    for copy in tables:
        copy.wait()

    @pl.loop(0, SEG)
    def _(s):
        seg_copy(0, s).wait_recv()
        seg_copy(1, s).start()

        @pl.when(s < SEG - EARLY)
        def _():
            seg_copy(0, s + EARLY).start()

        @pl.when(s > 0)
        def _():
            seg_copy(2, s - 1).wait_recv()
            own_dft(m2, s - 1, 0, CH)
            seg_copy(1, s - 1).wait_recv()
            window_dft(p2, s - 1, (2 * CH, 4 * CH))

            @pl.loop(0, CH // 8)
            def _(g):
                tr, ti = pair_sums(g)
                for j in range(NOFF):
                    accr[slot(g, j), :] = tr[j]
                    acci[slot(g, j), :] = ti[j]

        first_dfts(s)

    keep_copy(1).wait_recv()
    keep_copy(2).wait_recv()
    keep_left[pl.ds(CH, CH), :] = km2[...].astype(f32)
    keep_near[pl.ds(0, CH), :] = kv[...].astype(f32)
    for base in (CH, 3 * CH):
        keep_near[pl.ds(base, CH), :] = k1[...].astype(f32)
    for base in (2 * CH, 4 * CH):
        keep_near[pl.ds(base, CH), :] = k2[...].astype(f32)

    @pl.loop(0, CH // 8)
    def _(g):
        r0 = pl.multiple_of(g * 8, 8)
        a = keep_left[pl.ds(r0, 8), :]
        c = keep_left[pl.ds(CH + r0, 8), :]
        for j in range(NOFF):
            near = keep_near[pl.ds(r0 + offs[j], 8), :]
            scale[slot(g, j), :] = jnp.where(away(j, r0), c, a) * near

    ones = jnp.ones((BLK, BLK), b16)
    number = jnp.dot(scale[...].astype(b16), ones, preferred_element_type=f32)
    scale[...] = 1.0 / (jnp.maximum(number, 1.0) * math.sqrt(SAMP))

    def back_copy(q):
        rows = pl.ds(q * per * NOFF, per * NOFF)
        return remote(res_send.at[rows], res_recv.at[rows], 3, q, -2)

    def lags(re, im):
        spec = jnp.concatenate([re, im], axis=1)
        hi = spec.astype(b16)
        lo = (spec - hi.astype(f32)).astype(b16)
        y = jnp.dot(jnp.concatenate([hi, lo], axis=1), t_inv[...], preferred_element_type=f32)
        return y[:, :NLAG] + y[:, NLAG:]

    def sum_copy(src, got, sem, k, to):
        return pltpu.make_async_remote_copy(
            src_ref=src,
            dst_ref=got.at[k],
            send_sem=sem.at[0, k],
            recv_sem=sem.at[1, k],
            device_id=to,
            device_id_type=MESH,
        )

    seg_copy(2, SEG - 1).wait_recv()
    own_dft(m2, SEG - 1, 0, CH)
    seg_copy(1, SEG - 1).wait_recv()
    window_dft(p2, SEG - 1, (2 * CH, 4 * CH))

    def finish(g, sums):
        tr, ti = pair_sums(g)
        new = []
        for j in range(NOFF):
            by = scale[slot(g, j), :]
            tr[j] = tr[j] * by
            ti[j] = ti[j] * by
            accr[slot(g, j), :] = tr[j]
            acci[slot(g, j), :] = ti[j]
        return [t + u for t, u in zip(sums, tr + ti)]

    zero = jnp.zeros((8, BLK), f32)
    sums = lax.fori_loop(0, CH // 8, finish, [zero] * (2 * NOFF))
    sums = [jnp.sum(t, axis=0, keepdims=True) for t in sums]
    part[...] = lags(jnp.concatenate(sums[:NOFF], axis=0), jnp.concatenate(sums[NOFF:], axis=0))
    for k in range(1, ng):
        sum_copy(part, got_a, asem, k, along_grp(k)).start()

    for q in range(QUART):
        at = pl.ds(q * per * NOFF, per * NOFF)
        corr = lags(accr[at, :], acci[at, :])
        res[at, :] = corr
        res_send[at, :] = corr.astype(b16)
        back_copy(q).start()

    got_a[0] = part[...]
    for k in range(1, ng):
        sum_copy(part, got_a, asem, k, along_grp(k)).wait_recv()
    got_b[0] = jnp.sum(got_a[...], axis=0)
    for k in range(1, nd):
        sum_copy(got_b.at[0], got_b, bsem, k, along_dev(k)).start()

    for q in range(QUART):
        back_copy(q).wait_recv()
        for j in range(NOFF):
            at = pl.ds((q * NOFF + j) * per, per)
            mine = res[at, :]
            theirs = res_recv[at, :].astype(f32)
            for h in range(per // 8):
                r0 = q * per + h * 8
                val = jnp.where(away(j, r0), theirs[h * 8 : h * 8 + 8], mine[h * 8 : h * 8 + 8])
                out[pl.ds(r0 * NOFF + j, 8, stride=NOFF), :] = val

    for k in range(1, nd):
        sum_copy(got_b.at[0], got_b, bsem, k, along_dev(k)).wait_recv()
    stack[...] = jnp.sum(got_b[...], axis=0) * (1.0 / math.sqrt(CH * nd * ng))

    for k in range(1, ng):
        sum_copy(part, got_a, asem, k, along_grp(k)).wait_send()
    for k in range(1, nd):
        sum_copy(got_b.at[0], got_b, bsem, k, along_dev(k)).wait_send()
    for q in range(QUART):
        back_copy(q).wait_send()

    @pl.loop(0, SEG)
    def _(s):
        for line in range(3):
            seg_copy(line, s).wait_send()

    for line in range(3):
        keep_copy(line).wait_send()


def local(shape, series, taps, keep, offsets):
    ng, nd = shape
    f32, b16 = jnp.float32, jnp.bfloat16
    ser = jnp.transpose(series, (1, 0, 2))
    keep_rows = jnp.transpose(keep, (1, 0))
    vmem = pl.BlockSpec(memory_space=pltpu.VMEM)
    smem = pl.BlockSpec(memory_space=pltpu.SMEM)
    hbm = pl.BlockSpec(memory_space=pltpu.HBM)
    pairs = CH * NOFF
    vm = pltpu.VMEM
    corr, stack = pl.pallas_call(
        functools.partial(kernel, shape),
        out_shape=(
            jax.ShapeDtypeStruct((pairs, NLAG), f32),
            jax.ShapeDtypeStruct((NOFF, NLAG), f32),
        ),
        in_specs=[hbm, hbm, hbm, smem, hbm, hbm, hbm],
        out_specs=(vmem, vmem),
        scratch_shapes=[
            vm((SEG, CH, SAMP), b16),
            vm((CH, TAPS), b16),
            vm((SEG, CH), jnp.int32),
            vm((2 * BLK, 2 * BLK), b16),
            vm((4 * BLK, 2 * BLK), b16),
            vm((4 * BLK, 2 * NLAG), b16),
            vm((SEG, NB + 2, CH, BLK), b16),
            vm((SEG, NB + 2, CH, BLK), b16),
            vm((SEG, NB + 2, CH, BLK), b16),
            vm((SEG, NB, CH, BLK), b16),
            vm((CH, BLK), b16),
            vm((CH, BLK), b16),
            vm((CH, BLK), b16),
            vm((CH, BLK), b16),
            vm((BLK, BLK), f32),
            vm((CH, BLK), f32),
            vm((SEG * 9 * GRP_CH, BLK), f32),
            vm((EXT, BLK), f32),
            vm((2 * CH, BLK), f32),
            vm((NB * 2 * CH, BLK), f32),
            vm((NB * 2 * CH, BLK), f32),
            vm((NB * EXT, BLK), f32),
            vm((NB * EXT, BLK), f32),
            vm((pairs, BLK), f32),
            vm((pairs, BLK), f32),
            vm((pairs, BLK), f32),
            vm((pairs, NLAG), f32),
            vm((pairs, NLAG), b16),
            vm((pairs, NLAG), b16),
            vm((NOFF, NLAG), f32),
            vm((ng, NOFF, NLAG), f32),
            vm((nd, NOFF, NLAG), f32),
            pltpu.SemaphoreType.DMA((4, SEG + 1)),
            pltpu.SemaphoreType.DMA((4, SEG + 1)),
            pltpu.SemaphoreType.DMA((2, ng)),
            pltpu.SemaphoreType.DMA((2, nd)),
            pltpu.SemaphoreType.DMA((CH // GRP_CH + 5,)),
        ],
        compiler_params=pltpu.CompilerParams(
            collective_id=0, has_side_effects=True, vmem_limit_bytes=60 << 20
        ),
        name="whiten_correlate",
    )(ser, taps, keep_rows, offsets, *dft_tables())
    return corr.reshape(CH, NOFF, NLAG), stack


def solution(mesh):
    spec3 = P(("grp", "dev"), None, None)
    spec2 = P(("grp", "dev"), None)
    shape = (mesh.shape["grp"], mesh.shape["dev"])
    return jax.shard_map(
        functools.partial(local, shape),
        mesh=mesh,
        in_specs=(spec3, spec2, spec2, P()),
        out_specs=(spec3, P()),
        check_vma=False,
    )
```

```python
import functools
import math

import jax
import jax.numpy as jnp
import numpy as np
from jax import lax
from jax.experimental import pallas as pl
from jax.experimental.pallas import tpu as pltpu
from jax.sharding import PartitionSpec as P

SEG = 6
SAMP = 1024
BLK = 128
TAPS = 64
NLAG = 128
NOFF = 8
CH = 64
NB = SAMP // BLK
NEAR = 3 * CH
EXT = 5 * CH
GRP_CH = 16
ROWS = NB * CH
QUART = 4
STAGES = 2
EARLY = 3
LAG = 2
PEERS = 16
MESH = pl.DeviceIdType.MESH


def split(t):
    t32 = t.astype(np.float32)
    hi = t32.astype(jnp.bfloat16)
    lo = (t32 - hi.astype(np.float32)).astype(jnp.bfloat16)
    return hi, lo


def dft_tables():
    n = np.arange(2 * BLK, dtype=np.float64)[:, None]
    f = np.arange(BLK, dtype=np.float64)[None, :] + 0.5
    ang = 2.0 * np.pi * f * n / (2 * BLK)
    full = np.concatenate([np.cos(ang), -np.sin(ang)], axis=1)
    half = BLK // 2
    own = full[:BLK]
    win = np.concatenate([full[half : half + BLK], full[half + BLK :], full[:half]], axis=0)
    m = np.arange(NLAG, dtype=np.float64)[None, :]
    ang_inv = 2.0 * np.pi * f.T * m / (2 * BLK)
    inv_hi, inv_lo = split(np.concatenate([np.cos(ang_inv), -np.sin(ang_inv)], axis=0) / BLK)
    inv = np.concatenate(
        [
            np.concatenate([inv_hi, inv_lo], axis=1),
            np.concatenate([inv_hi, np.zeros_like(inv_lo)], axis=1),
        ],
        axis=0,
    )
    return np.concatenate(split(own), axis=0), np.concatenate(split(win), axis=0), inv


def kernel(
    shape,
    ser_hbm,
    taps_hbm,
    keep_hbm,
    offs,
    own_hbm,
    win_hbm,
    inv_hbm,
    out,
    stack,
    ser,
    taps_in,
    keep_in,
    t_own,
    t_win,
    t_inv,
    white,
    p1,
    p2,
    m2,
    kv,
    k1,
    k2,
    km2,
    kt,
    tk,
    scr,
    keep_near,
    keep_left,
    xr,
    xi,
    yr,
    yi,
    accr,
    acci,
    scale,
    res,
    res_send,
    res_recv,
    got,
    ssem,
    rsem,
    qsem,
    lsem,
):
    ng, nd = shape
    f32, b16 = jnp.float32, jnp.bfloat16
    me_g, me_d = lax.axis_index("grp"), lax.axis_index("dev")

    def dev(k):
        t = lax.rem(me_g * nd + me_d + (k + ng * nd), ng * nd)
        return (t // nd, lax.rem(t, nd))

    core, my_y = lax.rem(me_g, 2), lax.rem(me_g // 2, 4)
    x_hi, x_lo = me_g // 8, me_d // 8
    z = lax.rem(me_d, 8)

    def peer(stage, k):
        c, yy, xh, xl, zz = core, my_y, x_hi, x_lo, z
        if stage == 0:
            yy = lax.rem(my_y + k // 4, 4)
            xh, xl = lax.rem(x_hi + k // 2 % 2, 2), lax.rem(x_lo + k % 2, 2)
        else:
            zz, c = lax.rem(z + k // 2, 8), lax.rem(core + k % 2, 2)
        return ((xh * 4 + yy) * 2 + c, xl * 8 + zz)

    bar = pltpu.get_barrier_semaphore()
    for k in (-2, -1, 1, 2):
        pl.semaphore_signal(bar, inc=1, device_id=dev(k), device_id_type=MESH)

    groups = CH // GRP_CH
    small = [
        pltpu.make_async_copy(taps_hbm, taps_in, lsem.at[groups]),
        pltpu.make_async_copy(keep_hbm, keep_in, lsem.at[groups + 1]),
    ]
    loads = [
        pltpu.make_async_copy(
            ser_hbm.at[:, pl.ds(g * GRP_CH, GRP_CH), :],
            ser.at[:, pl.ds(g * GRP_CH, GRP_CH), :],
            lsem.at[g],
        )
        for g in range(groups)
    ]
    tables = [
        pltpu.make_async_copy(src, dst, lsem.at[groups + 2 + i])
        for i, (src, dst) in enumerate(((own_hbm, t_own), (win_hbm, t_win), (inv_hbm, t_inv)))
    ]
    for copy in small + loads + tables:
        copy.start()

    for stage in range(STAGES):
        for k in range(1, PEERS):
            pl.semaphore_signal(bar, inc=1, device_id=peer(stage, k), device_id_type=MESH)

    kt[...] = jnp.zeros_like(kt)
    tk[...] = jnp.zeros_like(tk)
    for s in range(SEG):
        scr[pl.ds(s * 9 * GRP_CH, GRP_CH), :] = jnp.zeros((GRP_CH, BLK), f32)
    for copy in small:
        copy.wait()
    tk[:, pl.ds(0, TAPS)] = taps_in[...].astype(f32)
    kt[pl.ds(0, SEG), pl.ds(0, CH)] = keep_in[...].astype(f32)
    flags = jnp.transpose(kt[...])[:CH]
    keep_left[pl.ds(0, CH), :] = flags
    kv[...] = flags.astype(b16)

    def remote(src, dst, line, at, to):
        return pltpu.make_async_remote_copy(
            src_ref=src,
            dst_ref=dst,
            send_sem=ssem.at[line, at],
            recv_sem=rsem.at[line, at],
            device_id=dev(to),
            device_id_type=MESH,
        )

    def keep_copy(line):
        if line == 0:
            return remote(kv, k1, 0, SEG, -1)
        if line == 1:
            return remote(k1, k2, 1, SEG, -1)
        return remote(kv, km2, 2, SEG, 2)

    def seg_copy(line, s, first=0, count=CH):
        blocks, rows = pl.ds(1, NB), pl.ds(first, count)
        if line == 0:
            return remote(white.at[s, blocks, rows], p1.at[s, blocks, rows], 0, s, -1)
        if line == 1:
            return remote(p1.at[s, blocks, rows], p2.at[s, blocks, rows], 1, s, -1)
        return remote(white.at[s, blocks, rows], m2.at[s, :, rows], 2, s, 2)

    row_i = lax.broadcasted_iota(jnp.int32, (BLK, BLK), 0)
    col_i = lax.broadcasted_iota(jnp.int32, (BLK, BLK), 1)
    causal = col_i >= row_i
    row_lane = lax.broadcasted_iota(jnp.int32, (1, BLK), 1)

    for g in range(groups):
        loads[g].wait()
        for s in range(SEG):
            for b in range(NB):
                x = ser[s, pl.ds(g * GRP_CH, GRP_CH), pl.ds(b * BLK, BLK)]
                scr[pl.ds((s * 9 + b + 1) * GRP_CH, GRP_CH), :] = x.astype(f32)

        @pl.loop(0, GRP_CH, unroll=2)
        def _(c):
            cur = [scr[pl.ds((s * 9 + 1) * GRP_CH + c, NB, stride=GRP_CH), :] for s in range(SEG)]
            prv = [scr[pl.ds(s * 9 * GRP_CH + c, NB, stride=GRP_CH), :] for s in range(SEG)]
            x = jnp.concatenate(
                [jnp.concatenate(prv, axis=0), jnp.concatenate(cur, axis=0)], axis=1
            ).astype(b16)
            row = tk[pl.ds(g * GRP_CH + c, 1), :]
            circ = pltpu.roll(jnp.broadcast_to(row, (BLK, BLK)), 0, 1, stride=1, stride_axis=0)
            toep = jnp.concatenate(
                [jnp.where(causal, 0.0, circ), jnp.where(causal, circ, 0.0)], axis=0
            ).astype(b16)
            y = jnp.dot(x, toep, preferred_element_type=f32)
            for s in range(SEG):
                scr[pl.ds((s * 9 + 1) * GRP_CH + c, NB, stride=GRP_CH), :] = y[s * NB : (s + 1) * NB]

        mine = keep_left[pl.ds(g * GRP_CH, GRP_CH), :]
        for s in range(SEG):
            flag = jnp.broadcast_to(mine[:, s : s + 1], (GRP_CH, BLK))
            for b in range(NB):
                y = scr[pl.ds((s * 9 + b + 1) * GRP_CH, GRP_CH), :] * flag
                white[s, b + 1, pl.ds(g * GRP_CH, GRP_CH), :] = y.astype(b16)
        if g == 0:
            pl.semaphore_wait(bar, 4 + STAGES * (PEERS - 1))
            keep_copy(0).start()
            keep_copy(2).start()
        for s in range(EARLY):
            seg_copy(0, s, g * GRP_CH, GRP_CH).start()
            seg_copy(2, s, g * GRP_CH, GRP_CH).start()

    for s in range(EARLY, SEG):
        seg_copy(2, s).start()
    keep_copy(0).wait_recv()
    keep_copy(1).start()

    for s in range(SEG):
        for ref in (white, p1, p2):
            ref[s, 0] = jnp.zeros((CH, BLK), b16)
            ref[s, NB + 1] = jnp.zeros((CH, BLK), b16)
    accr[...] = jnp.zeros_like(accr)
    acci[...] = jnp.zeros_like(acci)

    def window_dft(src, s, bases):
        nxt = jnp.where(row_lane < BLK // 2, 1.0, 0.0).astype(b16)
        prv = jnp.where(row_lane < BLK // 2, 0.0, 1.0).astype(b16)
        cur = src[s, pl.ds(1, NB)].reshape(ROWS, BLK)
        mix = src[s, pl.ds(2, NB)].reshape(ROWS, BLK) * nxt + src[s, pl.ds(0, NB)].reshape(ROWS, BLK) * prv
        x = jnp.concatenate([cur, mix, cur, mix], axis=1)
        y = jnp.dot(x, t_win[...], preferred_element_type=f32)
        for b in range(NB):
            for base in bases:
                yr[pl.ds(b * EXT + base, CH), :] = y[b * CH : (b + 1) * CH, :BLK]
                yi[pl.ds(b * EXT + base, CH), :] = y[b * CH : (b + 1) * CH, BLK:]

    def own_dft(src, s, start, base):
        w = src[s, pl.ds(start, NB)].reshape(ROWS, BLK)
        y = jnp.dot(jnp.concatenate([w, w], axis=1), t_own[...], preferred_element_type=f32)
        for b in range(NB):
            xr[pl.ds(b * 2 * CH + base, CH), :] = y[b * CH : (b + 1) * CH, :BLK]
            xi[pl.ds(b * 2 * CH + base, CH), :] = y[b * CH : (b + 1) * CH, BLK:]

    eight = lax.broadcasted_iota(jnp.int32, (8, BLK), 0)
    per = CH // QUART

    def away(j, r0):
        return eight + (r0 + offs[j]) >= NEAR

    def slot(g, j):
        first = (g // (per // 8)) * (per * NOFF) + lax.rem(g, per // 8) * 8
        return pl.ds(pl.multiple_of(first + j * per, 8), 8)

    def pair_sums(g):
        r0 = pl.multiple_of(g * 8, 8)
        far = [away(j, r0) for j in range(NOFF)]
        tr = [accr[slot(g, j), :] for j in range(NOFF)]
        ti = [acci[slot(g, j), :] for j in range(NOFF)]
        for b in range(NB):
            ar = xr[pl.ds(b * 2 * CH + r0, 8), :]
            ai = xi[pl.ds(b * 2 * CH + r0, 8), :]
            cr = xr[pl.ds(b * 2 * CH + CH + r0, 8), :]
            ci = xi[pl.ds(b * 2 * CH + CH + r0, 8), :]
            for j in range(NOFF):
                near = pl.ds(b * EXT + r0 + offs[j], 8)
                br = yr[near, :]
                bi = yi[near, :]
                lr = jnp.where(far[j], cr, ar)
                li = jnp.where(far[j], ci, ai)
                tr[j] = tr[j] + (lr * br + li * bi)
                ti[j] = ti[j] + (lr * bi - li * br)
        return tr, ti

    def first_dfts(s):
        own_dft(white, s, 1, 0)
        window_dft(white, s, (0,))
        window_dft(p1, s, (CH, 3 * CH))

    for copy in tables:
        copy.wait()

    def last_dfts(s):
        seg_copy(2, s).wait_recv()
        own_dft(m2, s, 0, CH)
        seg_copy(1, s).wait_recv()
        window_dft(p2, s, (2 * CH, 4 * CH))

    @pl.loop(0, SEG - 1 + LAG)
    def _(step):
        @pl.when(step < SEG)
        def _():
            seg_copy(0, step).wait_recv()
            seg_copy(1, step).start()

        @pl.when(step < SEG - EARLY)
        def _():
            seg_copy(0, step + EARLY).start()

        @pl.when(step >= LAG)
        def _():
            first_dfts(step - LAG)
            last_dfts(step - LAG)

            @pl.loop(0, CH // 8)
            def _(g):
                tr, ti = pair_sums(g)
                for j in range(NOFF):
                    accr[slot(g, j), :] = tr[j]
                    acci[slot(g, j), :] = ti[j]

    first_dfts(SEG - 1)

    keep_copy(1).wait_recv()
    keep_copy(2).wait_recv()
    keep_left[pl.ds(CH, CH), :] = km2[...].astype(f32)
    keep_near[pl.ds(0, CH), :] = kv[...].astype(f32)
    for base in (CH, 3 * CH):
        keep_near[pl.ds(base, CH), :] = k1[...].astype(f32)
    for base in (2 * CH, 4 * CH):
        keep_near[pl.ds(base, CH), :] = k2[...].astype(f32)

    @pl.loop(0, CH // 8)
    def _(g):
        r0 = pl.multiple_of(g * 8, 8)
        a = keep_left[pl.ds(r0, 8), :]
        c = keep_left[pl.ds(CH + r0, 8), :]
        for j in range(NOFF):
            near = keep_near[pl.ds(r0 + offs[j], 8), :]
            scale[slot(g, j), :] = jnp.where(away(j, r0), c, a) * near

    ones = jnp.ones((BLK, BLK), b16)
    number = jnp.dot(scale[...].astype(b16), ones, preferred_element_type=f32)
    scale[...] = 1.0 / (jnp.maximum(number, 1.0) * math.sqrt(SAMP))

    def back_copy(q):
        rows = pl.ds(q * per * NOFF, per * NOFF)
        return remote(res_send.at[rows], res_recv.at[rows], 3, q, -2)

    def lags(re, im):
        spec = jnp.concatenate([re, im], axis=1)
        hi = spec.astype(b16)
        lo = (spec - hi.astype(f32)).astype(b16)
        y = jnp.dot(jnp.concatenate([hi, lo], axis=1), t_inv[...], preferred_element_type=f32)
        return y[:, :NLAG] + y[:, NLAG:]

    def sum_copy(stage, k):
        return pltpu.make_async_remote_copy(
            src_ref=got.at[stage, 0],
            dst_ref=got.at[stage, k],
            send_sem=qsem.at[0, stage, k],
            recv_sem=qsem.at[1, stage, k],
            device_id=peer(stage, k),
            device_id_type=MESH,
        )

    def sum_start(stage):
        for k in range(1, PEERS):
            sum_copy(stage, k).start()

    def sum_wait(stage):
        for k in range(1, PEERS):
            sum_copy(stage, k).wait_recv()
        return jnp.sum(got[stage], axis=0)

    last_dfts(SEG - 1)

    def finish(g, sums):
        tr, ti = pair_sums(g)
        new = []
        for j in range(NOFF):
            by = scale[slot(g, j), :]
            tr[j] = tr[j] * by
            ti[j] = ti[j] * by
            accr[slot(g, j), :] = tr[j]
            acci[slot(g, j), :] = ti[j]
        return [t + u for t, u in zip(sums, tr + ti)]

    zero = jnp.zeros((8, BLK), f32)
    sums = lax.fori_loop(0, CH // 8, finish, [zero] * (2 * NOFF))
    sums = [jnp.sum(t, axis=0, keepdims=True) for t in sums]
    part = lags(jnp.concatenate(sums[:NOFF], axis=0), jnp.concatenate(sums[NOFF:], axis=0))
    got[0, 0] = part
    sum_start(0)

    for q in range(QUART):
        at = pl.ds(q * per * NOFF, per * NOFF)
        corr = lags(accr[at, :], acci[at, :])
        res[at, :] = corr
        res_send[at, :] = corr.astype(b16)
        back_copy(q).start()

    for stage in range(1, STAGES):
        got[stage, 0] = sum_wait(stage - 1)
        sum_start(stage)

    for q in range(QUART):
        back_copy(q).wait_recv()
        for j in range(NOFF):
            at = pl.ds((q * NOFF + j) * per, per)
            mine = res[at, :]
            theirs = res_recv[at, :].astype(f32)
            for h in range(per // 8):
                r0 = q * per + h * 8
                val = jnp.where(away(j, r0), theirs[h * 8 : h * 8 + 8], mine[h * 8 : h * 8 + 8])
                out[pl.ds(r0 * NOFF + j, 8, stride=NOFF), :] = val

    stack[...] = sum_wait(STAGES - 1) * (1.0 / math.sqrt(CH * nd * ng))
    for stage in range(STAGES):
        for k in range(1, PEERS):
            sum_copy(stage, k).wait_send()
    for q in range(QUART):
        back_copy(q).wait_send()

    @pl.loop(0, SEG)
    def _(s):
        for line in range(3):
            seg_copy(line, s).wait_send()

    for line in range(3):
        keep_copy(line).wait_send()


def local(shape, series, taps, keep, offsets):
    ng, nd = shape
    f32, b16 = jnp.float32, jnp.bfloat16
    ser = jnp.transpose(series, (1, 0, 2))
    keep_rows = jnp.transpose(keep, (1, 0))
    vmem = pl.BlockSpec(memory_space=pltpu.VMEM)
    smem = pl.BlockSpec(memory_space=pltpu.SMEM)
    hbm = pl.BlockSpec(memory_space=pltpu.HBM)
    pairs = CH * NOFF
    vm = pltpu.VMEM
    corr, stack = pl.pallas_call(
        functools.partial(kernel, shape),
        out_shape=(
            jax.ShapeDtypeStruct((pairs, NLAG), f32),
            jax.ShapeDtypeStruct((NOFF, NLAG), f32),
        ),
        in_specs=[hbm, hbm, hbm, smem, hbm, hbm, hbm],
        out_specs=(vmem, vmem),
        scratch_shapes=[
            vm((SEG, CH, SAMP), b16),
            vm((CH, TAPS), b16),
            vm((SEG, CH), jnp.int32),
            vm((2 * BLK, 2 * BLK), b16),
            vm((4 * BLK, 2 * BLK), b16),
            vm((4 * BLK, 2 * NLAG), b16),
            vm((SEG, NB + 2, CH, BLK), b16),
            vm((SEG, NB + 2, CH, BLK), b16),
            vm((SEG, NB + 2, CH, BLK), b16),
            vm((SEG, NB, CH, BLK), b16),
            vm((CH, BLK), b16),
            vm((CH, BLK), b16),
            vm((CH, BLK), b16),
            vm((CH, BLK), b16),
            vm((BLK, BLK), f32),
            vm((CH, BLK), f32),
            vm((SEG * 9 * GRP_CH, BLK), f32),
            vm((EXT, BLK), f32),
            vm((2 * CH, BLK), f32),
            vm((NB * 2 * CH, BLK), f32),
            vm((NB * 2 * CH, BLK), f32),
            vm((NB * EXT, BLK), f32),
            vm((NB * EXT, BLK), f32),
            vm((pairs, BLK), f32),
            vm((pairs, BLK), f32),
            vm((pairs, BLK), f32),
            vm((pairs, NLAG), f32),
            vm((pairs, NLAG), b16),
            vm((pairs, NLAG), b16),
            vm((STAGES, PEERS, NOFF, NLAG), f32),
            pltpu.SemaphoreType.DMA((4, SEG + 1)),
            pltpu.SemaphoreType.DMA((4, SEG + 1)),
            pltpu.SemaphoreType.DMA((2, STAGES, PEERS)),
            pltpu.SemaphoreType.DMA((CH // GRP_CH + 5,)),
        ],
        compiler_params=pltpu.CompilerParams(
            collective_id=0, has_side_effects=True, vmem_limit_bytes=60 << 20
        ),
        name="whiten_correlate",
    )(ser, taps, keep_rows, offsets, *dft_tables())
    return corr.reshape(CH, NOFF, NLAG), stack


def solution(mesh):
    spec3 = P(("grp", "dev"), None, None)
    spec2 = P(("grp", "dev"), None)
    shape = (mesh.shape["grp"], mesh.shape["dev"])
    return jax.shard_map(
        functools.partial(local, shape),
        mesh=mesh,
        in_specs=(spec3, spec2, spec2, P()),
        out_specs=(spec3, P()),
        check_vma=False,
    )
```

```python
import functools
import math

import jax
import jax.numpy as jnp
import numpy as np
from jax import lax
from jax.experimental import pallas as pl
from jax.experimental.pallas import tpu as pltpu
from jax.sharding import PartitionSpec as P

SEG = 6
SAMP = 1024
BLK = 128
TAPS = 64
NLAG = 128
NOFF = 8
CH = 64
NB = SAMP // BLK
NEAR = 3 * CH
EXT = 5 * CH
GRP_CH = 16
ROWS = NB * CH
QUART = 4
STAGES = 2
EARLY = 3
LAG = 3
PEERS = 16
FAR = (
    sorted(range(1, 16), key=lambda k: -(min(k // 4, 4 - k // 4) + (k // 2) % 2 * 2 + k % 2)),
    sorted(range(1, 16), key=lambda k: -min(k // 2, 8 - k // 2)),
)
MESH = pl.DeviceIdType.MESH


def split(t):
    t32 = t.astype(np.float32)
    hi = t32.astype(jnp.bfloat16)
    lo = (t32 - hi.astype(np.float32)).astype(jnp.bfloat16)
    return hi, lo


def dft_tables():
    n = np.arange(2 * BLK, dtype=np.float64)[:, None]
    f = np.arange(BLK, dtype=np.float64)[None, :] + 0.5
    ang = 2.0 * np.pi * f * n / (2 * BLK)
    full = np.concatenate([np.cos(ang), -np.sin(ang)], axis=1)
    half = BLK // 2
    own = full[:BLK]
    win = np.concatenate([full[half : half + BLK], full[half + BLK :], full[:half]], axis=0)
    m = np.arange(NLAG, dtype=np.float64)[None, :]
    ang_inv = 2.0 * np.pi * f.T * m / (2 * BLK)
    inv_hi, inv_lo = split(np.concatenate([np.cos(ang_inv), -np.sin(ang_inv)], axis=0) / BLK)
    inv = np.concatenate(
        [
            np.concatenate([inv_hi, inv_lo], axis=1),
            np.concatenate([inv_hi, np.zeros_like(inv_lo)], axis=1),
        ],
        axis=0,
    )
    return np.concatenate(split(own), axis=0), np.concatenate(split(win), axis=0), inv


def kernel(
    shape,
    ser_hbm,
    taps_hbm,
    keep_hbm,
    offs,
    own_hbm,
    win_hbm,
    inv_hbm,
    out_hbm,
    stack,
    ser,
    taps_in,
    keep_in,
    t_own,
    t_win,
    t_inv,
    white,
    p1,
    p2,
    m2,
    kv,
    k1,
    k2,
    km2,
    kt,
    tk,
    scr,
    keep_near,
    keep_left,
    xr,
    xi,
    yr,
    yi,
    accr,
    acci,
    scale,
    out,
    res,
    res_send,
    res_recv,
    got,
    ssem,
    rsem,
    qsem,
    lsem,
):
    ng, nd = shape
    f32, b16 = jnp.float32, jnp.bfloat16
    me_g, me_d = lax.axis_index("grp"), lax.axis_index("dev")

    def dev(k):
        t = lax.rem(me_g * nd + me_d + (k + ng * nd), ng * nd)
        return (t // nd, lax.rem(t, nd))

    core, my_y = lax.rem(me_g, 2), lax.rem(me_g // 2, 4)
    x_hi, x_lo = me_g // 8, me_d // 8
    z = lax.rem(me_d, 8)

    def peer(stage, k):
        c, yy, xh, xl, zz = core, my_y, x_hi, x_lo, z
        if stage == 0:
            yy = lax.rem(my_y + k // 4, 4)
            xh, xl = lax.rem(x_hi + k // 2 % 2, 2), lax.rem(x_lo + k % 2, 2)
        else:
            zz, c = lax.rem(z + k // 2, 8), lax.rem(core + k % 2, 2)
        return ((xh * 4 + yy) * 2 + c, xl * 8 + zz)

    bar = pltpu.get_barrier_semaphore()
    for k in (-2, -1, 1, 2):
        pl.semaphore_signal(bar, inc=1, device_id=dev(k), device_id_type=MESH)

    groups = CH // GRP_CH
    small = [
        pltpu.make_async_copy(taps_hbm, taps_in, lsem.at[groups]),
        pltpu.make_async_copy(keep_hbm, keep_in, lsem.at[groups + 1]),
    ]
    loads = [
        pltpu.make_async_copy(
            ser_hbm.at[:, pl.ds(g * GRP_CH, GRP_CH), :],
            ser.at[:, pl.ds(g * GRP_CH, GRP_CH), :],
            lsem.at[g],
        )
        for g in range(groups)
    ]
    tables = [
        pltpu.make_async_copy(src, dst, lsem.at[groups + 2 + i])
        for i, (src, dst) in enumerate(((own_hbm, t_own), (win_hbm, t_win), (inv_hbm, t_inv)))
    ]
    for copy in small + loads + tables:
        copy.start()

    for stage in range(STAGES):
        for k in range(1, PEERS):
            pl.semaphore_signal(bar, inc=1, device_id=peer(stage, k), device_id_type=MESH)

    kt[...] = jnp.zeros_like(kt)
    tk[...] = jnp.zeros_like(tk)
    for s in range(SEG):
        scr[pl.ds(s * 9 * GRP_CH, GRP_CH), :] = jnp.zeros((GRP_CH, BLK), f32)
    for copy in small:
        copy.wait()
    tk[:, pl.ds(0, TAPS)] = taps_in[...].astype(f32)
    kt[pl.ds(0, SEG), pl.ds(0, CH)] = keep_in[...].astype(f32)
    flags = jnp.transpose(kt[...])[:CH]
    keep_left[pl.ds(0, CH), :] = flags
    kv[...] = flags.astype(b16)

    def remote(src, dst, line, at, to):
        return pltpu.make_async_remote_copy(
            src_ref=src,
            dst_ref=dst,
            send_sem=ssem.at[line, at],
            recv_sem=rsem.at[line, at],
            device_id=dev(to),
            device_id_type=MESH,
        )

    def keep_copy(line):
        if line == 0:
            return remote(kv, k1, 0, SEG, -1)
        if line == 1:
            return remote(k1, k2, 1, SEG, -1)
        return remote(kv, km2, 2, SEG, 2)

    def seg_copy(line, s, first=0, count=CH):
        blocks, rows = pl.ds(1, NB), pl.ds(first, count)
        if line == 0:
            return remote(white.at[s, blocks, rows], p1.at[s, blocks, rows], 0, s, -1)
        if line == 1:
            return remote(p1.at[s, blocks, rows], p2.at[s, blocks, rows], 1, s, -1)
        return remote(white.at[s, blocks, rows], m2.at[s, :, rows], 2, s, 2)

    row_i = lax.broadcasted_iota(jnp.int32, (BLK, BLK), 0)
    col_i = lax.broadcasted_iota(jnp.int32, (BLK, BLK), 1)
    causal = col_i >= row_i
    row_lane = lax.broadcasted_iota(jnp.int32, (1, BLK), 1)

    for g in range(groups):
        loads[g].wait()
        for s in range(SEG):
            for b in range(NB):
                x = ser[s, pl.ds(g * GRP_CH, GRP_CH), pl.ds(b * BLK, BLK)]
                scr[pl.ds((s * 9 + b + 1) * GRP_CH, GRP_CH), :] = x.astype(f32)

        @pl.loop(0, GRP_CH, unroll=2)
        def _(c):
            cur = [scr[pl.ds((s * 9 + 1) * GRP_CH + c, NB, stride=GRP_CH), :] for s in range(SEG)]
            prv = [scr[pl.ds(s * 9 * GRP_CH + c, NB, stride=GRP_CH), :] for s in range(SEG)]
            x = jnp.concatenate(
                [jnp.concatenate(prv, axis=0), jnp.concatenate(cur, axis=0)], axis=1
            ).astype(b16)
            row = tk[pl.ds(g * GRP_CH + c, 1), :]
            circ = pltpu.roll(jnp.broadcast_to(row, (BLK, BLK)), 0, 1, stride=1, stride_axis=0)
            toep = jnp.concatenate(
                [jnp.where(causal, 0.0, circ), jnp.where(causal, circ, 0.0)], axis=0
            ).astype(b16)
            y = jnp.dot(x, toep, preferred_element_type=f32)
            for s in range(SEG):
                scr[pl.ds((s * 9 + 1) * GRP_CH + c, NB, stride=GRP_CH), :] = y[s * NB : (s + 1) * NB]

        mine = keep_left[pl.ds(g * GRP_CH, GRP_CH), :]
        for s in range(SEG):
            flag = jnp.broadcast_to(mine[:, s : s + 1], (GRP_CH, BLK))
            for b in range(NB):
                y = scr[pl.ds((s * 9 + b + 1) * GRP_CH, GRP_CH), :] * flag
                white[s, b + 1, pl.ds(g * GRP_CH, GRP_CH), :] = y.astype(b16)
        if g == 0:
            pl.semaphore_wait(bar, 4 + STAGES * (PEERS - 1))
            keep_copy(0).start()
            keep_copy(2).start()
        for s in range(EARLY):
            seg_copy(0, s, g * GRP_CH, GRP_CH).start()
            seg_copy(2, s, g * GRP_CH, GRP_CH).start()

    for s in range(EARLY, SEG):
        seg_copy(2, s).start()
    keep_copy(0).wait_recv()
    keep_copy(1).start()

    for s in range(SEG):
        for ref in (white, p1, p2):
            ref[s, 0] = jnp.zeros((CH, BLK), b16)
            ref[s, NB + 1] = jnp.zeros((CH, BLK), b16)
    accr[...] = jnp.zeros_like(accr)
    acci[...] = jnp.zeros_like(acci)

    def window_dft(src, s, turn, bases):
        nxt = jnp.where(row_lane < BLK // 2, 1.0, 0.0).astype(b16)
        prv = jnp.where(row_lane < BLK // 2, 0.0, 1.0).astype(b16)
        cur = src[s, pl.ds(1, NB)].reshape(ROWS, BLK)
        mix = src[s, pl.ds(2, NB)].reshape(ROWS, BLK) * nxt + src[s, pl.ds(0, NB)].reshape(ROWS, BLK) * prv
        x = jnp.concatenate([cur, mix, cur, mix], axis=1)
        y = jnp.dot(x, t_win[...], preferred_element_type=f32)
        for b in range(NB):
            for base in bases:
                yr[turn, pl.ds(b * EXT + base, CH), :] = y[b * CH : (b + 1) * CH, :BLK]
                yi[turn, pl.ds(b * EXT + base, CH), :] = y[b * CH : (b + 1) * CH, BLK:]

    def own_dft(src, s, turn, start, base):
        w = src[s, pl.ds(start, NB)].reshape(ROWS, BLK)
        y = jnp.dot(jnp.concatenate([w, w], axis=1), t_own[...], preferred_element_type=f32)
        for b in range(NB):
            xr[turn, pl.ds(b * 2 * CH + base, CH), :] = y[b * CH : (b + 1) * CH, :BLK]
            xi[turn, pl.ds(b * 2 * CH + base, CH), :] = y[b * CH : (b + 1) * CH, BLK:]

    eight = lax.broadcasted_iota(jnp.int32, (8, BLK), 0)
    per = CH // QUART

    def away(j, r0):
        return eight + (r0 + offs[j]) >= NEAR

    def slot(g, j):
        first = (g // (per // 8)) * (per * NOFF) + lax.rem(g, per // 8) * 8
        return pl.ds(pl.multiple_of(first + j * per, 8), 8)

    def pair_sums(turn, g):
        r0 = pl.multiple_of(g * 8, 8)
        far = [away(j, r0) for j in range(NOFF)]
        tr = [accr[slot(g, j), :] for j in range(NOFF)]
        ti = [acci[slot(g, j), :] for j in range(NOFF)]
        for b in range(NB):
            ar = xr[turn, pl.ds(b * 2 * CH + r0, 8), :]
            ai = xi[turn, pl.ds(b * 2 * CH + r0, 8), :]
            cr = xr[turn, pl.ds(b * 2 * CH + CH + r0, 8), :]
            ci = xi[turn, pl.ds(b * 2 * CH + CH + r0, 8), :]
            for j in range(NOFF):
                near = pl.ds(b * EXT + r0 + offs[j], 8)
                br = yr[turn, near, :]
                bi = yi[turn, near, :]
                lr = jnp.where(far[j], cr, ar)
                li = jnp.where(far[j], ci, ai)
                tr[j] = tr[j] + (lr * br + li * bi)
                ti[j] = ti[j] + (lr * bi - li * br)
        return tr, ti

    def first_dfts(s, turn):
        own_dft(white, s, turn, 1, 0)
        window_dft(white, s, turn, (0,))
        window_dft(p1, s, turn, (CH, 3 * CH))

    for copy in tables:
        copy.wait()

    def last_dfts(s, turn):
        seg_copy(2, s).wait_recv()
        own_dft(m2, s, turn, 0, CH)
        seg_copy(1, s).wait_recv()
        window_dft(p2, s, turn, (2 * CH, 4 * CH))

    @pl.loop(0, SEG - 1 + LAG)
    def _(step):
        @pl.when(step < SEG)
        def _():
            seg_copy(0, step).wait_recv()
            seg_copy(1, step).start()

        @pl.when(step < SEG - EARLY)
        def _():
            seg_copy(0, step + EARLY).start()

        @pl.when(step >= LAG)
        def _():
            turn = lax.rem(step - LAG, LAG)
            last_dfts(step - LAG, turn)

            @pl.loop(0, CH // 8)
            def _(g):
                tr, ti = pair_sums(turn, g)
                for j in range(NOFF):
                    accr[slot(g, j), :] = tr[j]
                    acci[slot(g, j), :] = ti[j]

        @pl.when(step < SEG)
        def _():
            first_dfts(step, lax.rem(step, LAG))

    keep_copy(1).wait_recv()
    keep_copy(2).wait_recv()
    keep_left[pl.ds(CH, CH), :] = km2[...].astype(f32)
    keep_near[pl.ds(0, CH), :] = kv[...].astype(f32)
    for base in (CH, 3 * CH):
        keep_near[pl.ds(base, CH), :] = k1[...].astype(f32)
    for base in (2 * CH, 4 * CH):
        keep_near[pl.ds(base, CH), :] = k2[...].astype(f32)

    @pl.loop(0, CH // 8)
    def _(g):
        r0 = pl.multiple_of(g * 8, 8)
        a = keep_left[pl.ds(r0, 8), :]
        c = keep_left[pl.ds(CH + r0, 8), :]
        for j in range(NOFF):
            near = keep_near[pl.ds(r0 + offs[j], 8), :]
            scale[slot(g, j), :] = jnp.where(away(j, r0), c, a) * near

    ones = jnp.ones((BLK, BLK), b16)
    number = jnp.dot(scale[...].astype(b16), ones, preferred_element_type=f32)
    scale[...] = 1.0 / (jnp.maximum(number, 1.0) * math.sqrt(SAMP))

    def back_copy(q):
        rows = pl.ds(q * per * NOFF, per * NOFF)
        return remote(res_send.at[rows], res_recv.at[rows], 3, q, -2)

    def out_copy(q):
        rows = pl.ds(q * per * NOFF, per * NOFF)
        return pltpu.make_async_copy(out.at[rows], out_hbm.at[rows], lsem.at[q])

    def lags(re, im):
        spec = jnp.concatenate([re, im], axis=1)
        hi = spec.astype(b16)
        lo = (spec - hi.astype(f32)).astype(b16)
        y = jnp.dot(jnp.concatenate([hi, lo], axis=1), t_inv[...], preferred_element_type=f32)
        return y[:, :NLAG] + y[:, NLAG:]

    def sum_copy(stage, k):
        return pltpu.make_async_remote_copy(
            src_ref=got.at[stage, 0],
            dst_ref=got.at[stage, k],
            send_sem=qsem.at[0, stage, k],
            recv_sem=qsem.at[1, stage, k],
            device_id=peer(stage, k),
            device_id_type=MESH,
        )

    def sum_start(stage):
        for k in FAR[stage]:
            sum_copy(stage, k).start()

    def sum_wait(stage):
        for k in range(1, PEERS):
            sum_copy(stage, k).wait_recv()
        return jnp.sum(got[stage], axis=0)

    turn = (SEG - 1) % LAG
    last_dfts(SEG - 1, turn)

    def finish(g, sums):
        tr, ti = pair_sums(turn, g)
        new = []
        for j in range(NOFF):
            by = scale[slot(g, j), :]
            tr[j] = tr[j] * by
            ti[j] = ti[j] * by
            accr[slot(g, j), :] = tr[j]
            acci[slot(g, j), :] = ti[j]
        return [t + u for t, u in zip(sums, tr + ti)]

    zero = jnp.zeros((8, BLK), f32)
    sums = lax.fori_loop(0, CH // 8, finish, [zero] * (2 * NOFF))
    sums = [jnp.sum(t, axis=0, keepdims=True) for t in sums]
    part = lags(jnp.concatenate(sums[:NOFF], axis=0), jnp.concatenate(sums[NOFF:], axis=0))
    got[0, 0] = part
    sum_start(0)

    for q in range(QUART):
        at = pl.ds(q * per * NOFF, per * NOFF)
        corr = lags(accr[at, :], acci[at, :])
        res[at, :] = corr
        res_send[at, :] = corr.astype(b16)
        back_copy(q).start()

    for stage in range(1, STAGES):
        got[stage, 0] = sum_wait(stage - 1)
        sum_start(stage)

    for q in range(QUART):
        back_copy(q).wait_recv()
        for j in range(NOFF):
            at = pl.ds((q * NOFF + j) * per, per)
            mine = res[at, :]
            theirs = res_recv[at, :].astype(f32)
            for h in range(per // 8):
                r0 = q * per + h * 8
                val = jnp.where(away(j, r0), theirs[h * 8 : h * 8 + 8], mine[h * 8 : h * 8 + 8])
                out[pl.ds(r0 * NOFF + j, 8, stride=NOFF), :] = val
        out_copy(q).start()

    stack[...] = sum_wait(STAGES - 1) * (1.0 / math.sqrt(CH * nd * ng))
    for stage in range(STAGES):
        for k in range(1, PEERS):
            sum_copy(stage, k).wait_send()
    for q in range(QUART):
        out_copy(q).wait()
        back_copy(q).wait_send()

    @pl.loop(0, SEG)
    def _(s):
        for line in range(3):
            seg_copy(line, s).wait_send()

    for line in range(3):
        keep_copy(line).wait_send()


def local(shape, series, taps, keep, offsets):
    ng, nd = shape
    f32, b16 = jnp.float32, jnp.bfloat16
    ser = jnp.transpose(series, (1, 0, 2))
    keep_rows = jnp.transpose(keep, (1, 0))
    vmem = pl.BlockSpec(memory_space=pltpu.VMEM)
    smem = pl.BlockSpec(memory_space=pltpu.SMEM)
    hbm = pl.BlockSpec(memory_space=pltpu.HBM)
    pairs = CH * NOFF
    vm = pltpu.VMEM
    corr, stack = pl.pallas_call(
        functools.partial(kernel, shape),
        out_shape=(
            jax.ShapeDtypeStruct((pairs, NLAG), f32),
            jax.ShapeDtypeStruct((NOFF, NLAG), f32),
        ),
        in_specs=[hbm, hbm, hbm, smem, hbm, hbm, hbm],
        out_specs=(hbm, vmem),
        scratch_shapes=[
            vm((SEG, CH, SAMP), b16),
            vm((CH, TAPS), b16),
            vm((SEG, CH), jnp.int32),
            vm((2 * BLK, 2 * BLK), b16),
            vm((4 * BLK, 2 * BLK), b16),
            vm((4 * BLK, 2 * NLAG), b16),
            vm((SEG, NB + 2, CH, BLK), b16),
            vm((SEG, NB + 2, CH, BLK), b16),
            vm((SEG, NB + 2, CH, BLK), b16),
            vm((SEG, NB, CH, BLK), b16),
            vm((CH, BLK), b16),
            vm((CH, BLK), b16),
            vm((CH, BLK), b16),
            vm((CH, BLK), b16),
            vm((BLK, BLK), f32),
            vm((CH, BLK), f32),
            vm((SEG * 9 * GRP_CH, BLK), f32),
            vm((EXT, BLK), f32),
            vm((2 * CH, BLK), f32),
            vm((LAG, NB * 2 * CH, BLK), f32),
            vm((LAG, NB * 2 * CH, BLK), f32),
            vm((LAG, NB * EXT, BLK), f32),
            vm((LAG, NB * EXT, BLK), f32),
            vm((pairs, BLK), f32),
            vm((pairs, BLK), f32),
            vm((pairs, BLK), f32),
            vm((pairs, NLAG), f32),
            vm((pairs, NLAG), f32),
            vm((pairs, NLAG), b16),
            vm((pairs, NLAG), b16),
            vm((STAGES, PEERS, NOFF, NLAG), f32),
            pltpu.SemaphoreType.DMA((4, SEG + 1)),
            pltpu.SemaphoreType.DMA((4, SEG + 1)),
            pltpu.SemaphoreType.DMA((2, STAGES, PEERS)),
            pltpu.SemaphoreType.DMA((CH // GRP_CH + 5,)),
        ],
        compiler_params=pltpu.CompilerParams(
            collective_id=0, has_side_effects=True, vmem_limit_bytes=60 << 20
        ),
        name="whiten_correlate",
    )(ser, taps, keep_rows, offsets, *dft_tables())
    return corr.reshape(CH, NOFF, NLAG), stack


def solution(mesh):
    spec3 = P(("grp", "dev"), None, None)
    spec2 = P(("grp", "dev"), None)
    shape = (mesh.shape["grp"], mesh.shape["dev"])
    return jax.shard_map(
        functools.partial(local, shape),
        mesh=mesh,
        in_specs=(spec3, spec2, spec2, P()),
        out_specs=(spec3, P()),
        check_vma=False,
    )
```

```python
import functools
import math

import jax
import jax.numpy as jnp
import numpy as np
from jax import lax
from jax.experimental import pallas as pl
from jax.experimental.pallas import tpu as pltpu
from jax.sharding import PartitionSpec as P

SEG = 6
SAMP = 1024
BLK = 128
TAPS = 64
NLAG = 128
NOFF = 8
CH = 64
NB = SAMP // BLK
NEAR = 3 * CH
EXT = 5 * CH
GRP_CH = 16
ROWS = NB * CH
QUART = 4
STAGES = 2
EARLY = 3
LAG = 3
PIECES = 4
PEERS = 16
FAR = (
    sorted(range(1, 16), key=lambda k: -(min(k // 4, 4 - k // 4) + (k // 2) % 2 * 2 + k % 2)),
    sorted(range(1, 16), key=lambda k: -min(k // 2, 8 - k // 2)),
)
MESH = pl.DeviceIdType.MESH


def split(t):
    t32 = t.astype(np.float32)
    hi = t32.astype(jnp.bfloat16)
    lo = (t32 - hi.astype(np.float32)).astype(jnp.bfloat16)
    return hi, lo


def dft_tables():
    n = np.arange(2 * BLK, dtype=np.float64)[:, None]
    f = np.arange(BLK, dtype=np.float64)[None, :] + 0.5
    ang = 2.0 * np.pi * f * n / (2 * BLK)
    full = np.concatenate([np.cos(ang), -np.sin(ang)], axis=1)
    half = BLK // 2
    own = full[:BLK]
    win = np.concatenate([full[half : half + BLK], full[half + BLK :], full[:half]], axis=0)
    m = np.arange(NLAG, dtype=np.float64)[None, :]
    ang_inv = 2.0 * np.pi * f.T * m / (2 * BLK)
    inv_hi, inv_lo = split(np.concatenate([np.cos(ang_inv), -np.sin(ang_inv)], axis=0) / BLK)
    inv = np.concatenate(
        [
            np.concatenate([inv_hi, inv_lo], axis=1),
            np.concatenate([inv_hi, np.zeros_like(inv_lo)], axis=1),
        ],
        axis=0,
    )
    return np.concatenate(split(own), axis=0), np.concatenate(split(win), axis=0), inv


def kernel(
    shape,
    ser_hbm,
    taps_hbm,
    keep_hbm,
    offs,
    own_hbm,
    win_hbm,
    inv_hbm,
    out_hbm,
    stack,
    ser,
    taps_in,
    keep_in,
    t_own,
    t_win,
    t_inv,
    white,
    p1,
    p2,
    m2,
    kv,
    k1,
    k2,
    km2,
    kt,
    tk,
    scr,
    keep_near,
    keep_left,
    xr,
    xi,
    yr,
    yi,
    accr,
    acci,
    scale,
    out,
    res,
    res_send,
    res_recv,
    got,
    ssem,
    rsem,
    qsem,
    lsem,
):
    ng, nd = shape
    f32, b16 = jnp.float32, jnp.bfloat16
    me_g, me_d = lax.axis_index("grp"), lax.axis_index("dev")

    def dev(k):
        t = lax.rem(me_g * nd + me_d + (k + ng * nd), ng * nd)
        return (t // nd, lax.rem(t, nd))

    core, my_y = lax.rem(me_g, 2), lax.rem(me_g // 2, 4)
    x_hi, x_lo = me_g // 8, me_d // 8
    z = lax.rem(me_d, 8)

    def peer(stage, k):
        c, yy, xh, xl, zz = core, my_y, x_hi, x_lo, z
        if stage == 0:
            yy = lax.rem(my_y + k // 4, 4)
            xh, xl = lax.rem(x_hi + k // 2 % 2, 2), lax.rem(x_lo + k % 2, 2)
        else:
            zz, c = lax.rem(z + k // 2, 8), lax.rem(core + k % 2, 2)
        return ((xh * 4 + yy) * 2 + c, xl * 8 + zz)

    bar = pltpu.get_barrier_semaphore()
    for k in (-2, -1, 1, 2):
        pl.semaphore_signal(bar, inc=1, device_id=dev(k), device_id_type=MESH)

    groups = CH // GRP_CH
    small = [
        pltpu.make_async_copy(taps_hbm, taps_in, lsem.at[groups]),
        pltpu.make_async_copy(keep_hbm, keep_in, lsem.at[groups + 1]),
    ]
    loads = [
        pltpu.make_async_copy(
            ser_hbm.at[:, pl.ds(g * GRP_CH, GRP_CH), :],
            ser.at[:, pl.ds(g * GRP_CH, GRP_CH), :],
            lsem.at[g],
        )
        for g in range(groups)
    ]
    tables = [
        pltpu.make_async_copy(src, dst, lsem.at[groups + 2 + i])
        for i, (src, dst) in enumerate(((own_hbm, t_own), (win_hbm, t_win), (inv_hbm, t_inv)))
    ]
    for copy in small + loads + tables:
        copy.start()

    for stage in range(STAGES):
        for k in range(1, PEERS):
            pl.semaphore_signal(bar, inc=1, device_id=peer(stage, k), device_id_type=MESH)

    kt[...] = jnp.zeros_like(kt)
    tk[...] = jnp.zeros_like(tk)
    for s in range(SEG):
        scr[pl.ds(s * 9 * GRP_CH, GRP_CH), :] = jnp.zeros((GRP_CH, BLK), f32)
    for copy in small:
        copy.wait()
    tk[:, pl.ds(0, TAPS)] = taps_in[...].astype(f32)
    kt[pl.ds(0, SEG), pl.ds(0, CH)] = keep_in[...].astype(f32)
    flags = jnp.transpose(kt[...])[:CH]
    keep_left[pl.ds(0, CH), :] = flags
    kv[...] = flags.astype(b16)

    def remote(src, dst, line, at, to):
        return pltpu.make_async_remote_copy(
            src_ref=src,
            dst_ref=dst,
            send_sem=ssem.at[line, at],
            recv_sem=rsem.at[line, at],
            device_id=dev(to),
            device_id_type=MESH,
        )

    def keep_copy(line):
        if line == 0:
            return remote(kv, k1, 0, SEG, -1)
        if line == 1:
            return remote(k1, k2, 1, SEG, -1)
        return remote(kv, km2, 2, SEG, 2)

    def seg_copy(line, s, first=0, count=CH):
        blocks, rows = pl.ds(1, NB), pl.ds(first, count)
        if line == 0:
            return remote(white.at[s, blocks, rows], p1.at[s, blocks, rows], 0, s, -1)
        if line == 1:
            return remote(p1.at[s, blocks, rows], p2.at[s, blocks, rows], 1, s, -1)
        return remote(white.at[s, blocks, rows], m2.at[s, :, rows], 2, s, 2)

    row_i = lax.broadcasted_iota(jnp.int32, (BLK, BLK), 0)
    col_i = lax.broadcasted_iota(jnp.int32, (BLK, BLK), 1)
    causal = col_i >= row_i
    row_lane = lax.broadcasted_iota(jnp.int32, (1, BLK), 1)

    for g in range(groups):
        loads[g].wait()
        for s in range(SEG):
            for b in range(NB):
                x = ser[s, pl.ds(g * GRP_CH, GRP_CH), pl.ds(b * BLK, BLK)]
                scr[pl.ds((s * 9 + b + 1) * GRP_CH, GRP_CH), :] = x.astype(f32)

        @pl.loop(0, GRP_CH, unroll=2)
        def _(c):
            cur = [scr[pl.ds((s * 9 + 1) * GRP_CH + c, NB, stride=GRP_CH), :] for s in range(SEG)]
            prv = [scr[pl.ds(s * 9 * GRP_CH + c, NB, stride=GRP_CH), :] for s in range(SEG)]
            x = jnp.concatenate(
                [jnp.concatenate(prv, axis=0), jnp.concatenate(cur, axis=0)], axis=1
            ).astype(b16)
            row = tk[pl.ds(g * GRP_CH + c, 1), :]
            circ = pltpu.roll(jnp.broadcast_to(row, (BLK, BLK)), 0, 1, stride=1, stride_axis=0)
            toep = jnp.concatenate(
                [jnp.where(causal, 0.0, circ), jnp.where(causal, circ, 0.0)], axis=0
            ).astype(b16)
            y = jnp.dot(x, toep, preferred_element_type=f32)
            for s in range(SEG):
                scr[pl.ds((s * 9 + 1) * GRP_CH + c, NB, stride=GRP_CH), :] = y[s * NB : (s + 1) * NB]

        mine = keep_left[pl.ds(g * GRP_CH, GRP_CH), :]
        for s in range(SEG):
            flag = jnp.broadcast_to(mine[:, s : s + 1], (GRP_CH, BLK))
            for b in range(NB):
                y = scr[pl.ds((s * 9 + b + 1) * GRP_CH, GRP_CH), :] * flag
                white[s, b + 1, pl.ds(g * GRP_CH, GRP_CH), :] = y.astype(b16)
        if g == 0:
            pl.semaphore_wait(bar, 4 + STAGES * (PEERS - 1))
            keep_copy(0).start()
            keep_copy(2).start()
        for s in range(EARLY):
            seg_copy(0, s, g * GRP_CH, GRP_CH).start()
            seg_copy(2, s, g * GRP_CH, GRP_CH).start()

    for s in range(EARLY, SEG):
        seg_copy(2, s).start()
    keep_copy(0).wait_recv()
    keep_copy(1).start()

    for s in range(SEG):
        for ref in (white, p1, p2):
            ref[s, 0] = jnp.zeros((CH, BLK), b16)
            ref[s, NB + 1] = jnp.zeros((CH, BLK), b16)
    accr[...] = jnp.zeros_like(accr)
    acci[...] = jnp.zeros_like(acci)

    def window_dft(src, s, turn, bases):
        nxt = jnp.where(row_lane < BLK // 2, 1.0, 0.0).astype(b16)
        prv = jnp.where(row_lane < BLK // 2, 0.0, 1.0).astype(b16)
        cur = src[s, pl.ds(1, NB)].reshape(ROWS, BLK)
        mix = src[s, pl.ds(2, NB)].reshape(ROWS, BLK) * nxt + src[s, pl.ds(0, NB)].reshape(ROWS, BLK) * prv
        x = jnp.concatenate([cur, mix, cur, mix], axis=1)
        y = jnp.dot(x, t_win[...], preferred_element_type=f32)
        for b in range(NB):
            for base in bases:
                yr[turn, pl.ds(b * EXT + base, CH), :] = y[b * CH : (b + 1) * CH, :BLK]
                yi[turn, pl.ds(b * EXT + base, CH), :] = y[b * CH : (b + 1) * CH, BLK:]

    def own_dft(src, s, turn, start, base):
        w = src[s, pl.ds(start, NB)].reshape(ROWS, BLK)
        y = jnp.dot(jnp.concatenate([w, w], axis=1), t_own[...], preferred_element_type=f32)
        for b in range(NB):
            xr[turn, pl.ds(b * 2 * CH + base, CH), :] = y[b * CH : (b + 1) * CH, :BLK]
            xi[turn, pl.ds(b * 2 * CH + base, CH), :] = y[b * CH : (b + 1) * CH, BLK:]

    eight = lax.broadcasted_iota(jnp.int32, (8, BLK), 0)
    per = CH // QUART

    def away(j, r0):
        return eight + (r0 + offs[j]) >= NEAR

    def slot(g, j):
        first = (g // (per // 8)) * (per * NOFF) + lax.rem(g, per // 8) * 8
        return pl.ds(pl.multiple_of(first + j * per, 8), 8)

    def pair_sums(turn, g):
        r0 = pl.multiple_of(g * 8, 8)
        far = [away(j, r0) for j in range(NOFF)]
        tr = [accr[slot(g, j), :] for j in range(NOFF)]
        ti = [acci[slot(g, j), :] for j in range(NOFF)]
        for b in range(NB):
            ar = xr[turn, pl.ds(b * 2 * CH + r0, 8), :]
            ai = xi[turn, pl.ds(b * 2 * CH + r0, 8), :]
            cr = xr[turn, pl.ds(b * 2 * CH + CH + r0, 8), :]
            ci = xi[turn, pl.ds(b * 2 * CH + CH + r0, 8), :]
            for j in range(NOFF):
                near = pl.ds(b * EXT + r0 + offs[j], 8)
                br = yr[turn, near, :]
                bi = yi[turn, near, :]
                lr = jnp.where(far[j], cr, ar)
                li = jnp.where(far[j], ci, ai)
                tr[j] = tr[j] + (lr * br + li * bi)
                ti[j] = ti[j] + (lr * bi - li * br)
        return tr, ti

    def first_dfts(s, turn):
        own_dft(white, s, turn, 1, 0)
        window_dft(white, s, turn, (0,))
        window_dft(p1, s, turn, (CH, 3 * CH))

    for copy in tables:
        copy.wait()

    def last_dfts(s, turn):
        seg_copy(2, s).wait_recv()
        own_dft(m2, s, turn, 0, CH)
        seg_copy(1, s).wait_recv()
        window_dft(p2, s, turn, (2 * CH, 4 * CH))

    @pl.loop(0, SEG - 1 + LAG)
    def _(step):
        @pl.when(step < SEG)
        def _():
            seg_copy(0, step).wait_recv()
            seg_copy(1, step).start()

        @pl.when(step < SEG - EARLY)
        def _():
            seg_copy(0, step + EARLY).start()

        @pl.when(step >= LAG)
        def _():
            turn = lax.rem(step - LAG, LAG)
            last_dfts(step - LAG, turn)

            @pl.loop(0, CH // 8)
            def _(g):
                tr, ti = pair_sums(turn, g)
                for j in range(NOFF):
                    accr[slot(g, j), :] = tr[j]
                    acci[slot(g, j), :] = ti[j]

        @pl.when(step < SEG)
        def _():
            first_dfts(step, lax.rem(step, LAG))

    keep_copy(1).wait_recv()
    keep_copy(2).wait_recv()
    keep_left[pl.ds(CH, CH), :] = km2[...].astype(f32)
    keep_near[pl.ds(0, CH), :] = kv[...].astype(f32)
    for base in (CH, 3 * CH):
        keep_near[pl.ds(base, CH), :] = k1[...].astype(f32)
    for base in (2 * CH, 4 * CH):
        keep_near[pl.ds(base, CH), :] = k2[...].astype(f32)

    @pl.loop(0, CH // 8)
    def _(g):
        r0 = pl.multiple_of(g * 8, 8)
        a = keep_left[pl.ds(r0, 8), :]
        c = keep_left[pl.ds(CH + r0, 8), :]
        for j in range(NOFF):
            near = keep_near[pl.ds(r0 + offs[j], 8), :]
            scale[slot(g, j), :] = jnp.where(away(j, r0), c, a) * near

    ones = jnp.ones((BLK, BLK), b16)
    number = jnp.dot(scale[...].astype(b16), ones, preferred_element_type=f32)
    scale[...] = 1.0 / (jnp.maximum(number, 1.0) * math.sqrt(SAMP))

    def back_copy(q):
        rows = pl.ds(q * per * NOFF, per * NOFF)
        return remote(res_send.at[rows], res_recv.at[rows], 3, q, -2)

    def out_copy(q):
        rows = pl.ds(q * per * NOFF, per * NOFF)
        return pltpu.make_async_copy(out.at[rows], out_hbm.at[rows], lsem.at[q])

    def lags(re, im):
        spec = jnp.concatenate([re, im], axis=1)
        hi = spec.astype(b16)
        lo = (spec - hi.astype(f32)).astype(b16)
        y = jnp.dot(jnp.concatenate([hi, lo], axis=1), t_inv[...], preferred_element_type=f32)
        return y[:, :NLAG] + y[:, NLAG:]

    def sum_copy(stage, k):
        return pltpu.make_async_remote_copy(
            src_ref=got.at[stage, 0],
            dst_ref=got.at[stage, k],
            send_sem=qsem.at[0, stage, k],
            recv_sem=qsem.at[1, stage, k],
            device_id=peer(stage, k),
            device_id_type=MESH,
        )

    def sum_start(stage):
        for k in FAR[stage]:
            sum_copy(stage, k).start()

    def sum_wait(stage):
        for k in range(1, PEERS):
            sum_copy(stage, k).wait_recv()
        return jnp.sum(got[stage], axis=0)

    turn = (SEG - 1) % LAG
    last_dfts(SEG - 1, turn)

    def finish(g, sums):
        tr, ti = pair_sums(turn, g)
        new = []
        for j in range(NOFF):
            by = scale[slot(g, j), :]
            tr[j] = tr[j] * by
            ti[j] = ti[j] * by
            accr[slot(g, j), :] = tr[j]
            acci[slot(g, j), :] = ti[j]
        return [t + u for t, u in zip(sums, tr + ti)]

    zero = jnp.zeros((8, BLK), f32)
    sums = lax.fori_loop(0, CH // 8, finish, [zero] * (2 * NOFF))
    sums = [jnp.sum(t, axis=0, keepdims=True) for t in sums]
    part = lags(jnp.concatenate(sums[:NOFF], axis=0), jnp.concatenate(sums[NOFF:], axis=0))
    got[0, 0] = part
    sum_start(0)

    for q in range(QUART):
        at = pl.ds(q * per * NOFF, per * NOFF)
        corr = lags(accr[at, :], acci[at, :])
        res[at, :] = corr
        res_send[at, :] = corr.astype(b16)
        back_copy(q).start()

    for stage in range(1, STAGES):
        got[stage, 0] = sum_wait(stage - 1)
        sum_start(stage)

    for q in range(QUART):
        back_copy(q).wait_recv()
        for j in range(NOFF):
            at = pl.ds((q * NOFF + j) * per, per)
            mine = res[at, :]
            theirs = res_recv[at, :].astype(f32)
            for h in range(per // 8):
                r0 = q * per + h * 8
                val = jnp.where(away(j, r0), theirs[h * 8 : h * 8 + 8], mine[h * 8 : h * 8 + 8])
                out[pl.ds(r0 * NOFF + j, 8, stride=NOFF), :] = val
        out_copy(q).start()

    stack[...] = sum_wait(STAGES - 1) * (1.0 / math.sqrt(CH * nd * ng))
    for stage in range(STAGES):
        for k in range(1, PEERS):
            sum_copy(stage, k).wait_send()
    for q in range(QUART):
        out_copy(q).wait()
        back_copy(q).wait_send()

    @pl.loop(0, SEG)
    def _(s):
        for line in range(3):
            seg_copy(line, s).wait_send()

    for line in range(3):
        keep_copy(line).wait_send()


def hand_over(corr_in, stack_in, corr, stack, held, small, sem):
    rows = CH * NOFF // PIECES
    parts = [pl.ds(i * rows, rows) for i in range(PIECES)]
    inward = [
        pltpu.make_async_copy(corr_in.at[p], held.at[p], sem.at[0, i]) for i, p in enumerate(parts)
    ]
    inward.append(pltpu.make_async_copy(stack_in, small, sem.at[0, PIECES]))
    outward = [
        pltpu.make_async_copy(held.at[p], corr.at[p], sem.at[1, i]) for i, p in enumerate(parts)
    ]
    outward.append(pltpu.make_async_copy(small, stack, sem.at[1, PIECES]))
    for copy in inward:
        copy.start()
    for arrived, leaving in zip(inward, outward):
        arrived.wait()
        leaving.start()
    for copy in outward:
        copy.wait()


def local(shape, series, taps, keep, offsets):
    ng, nd = shape
    f32, b16 = jnp.float32, jnp.bfloat16
    ser = jnp.transpose(series, (1, 0, 2))
    keep_rows = jnp.transpose(keep, (1, 0))
    vmem = pl.BlockSpec(memory_space=pltpu.VMEM)
    smem = pl.BlockSpec(memory_space=pltpu.SMEM)
    hbm = pl.BlockSpec(memory_space=pltpu.HBM)
    pairs = CH * NOFF
    vm = pltpu.VMEM
    corr, stack = pl.pallas_call(
        functools.partial(kernel, shape),
        out_shape=(
            jax.ShapeDtypeStruct((pairs, NLAG), f32),
            jax.ShapeDtypeStruct((NOFF, NLAG), f32),
        ),
        in_specs=[hbm, hbm, hbm, smem, hbm, hbm, hbm],
        out_specs=(hbm, vmem),
        scratch_shapes=[
            vm((SEG, CH, SAMP), b16),
            vm((CH, TAPS), b16),
            vm((SEG, CH), jnp.int32),
            vm((2 * BLK, 2 * BLK), b16),
            vm((4 * BLK, 2 * BLK), b16),
            vm((4 * BLK, 2 * NLAG), b16),
            vm((SEG, NB + 2, CH, BLK), b16),
            vm((SEG, NB + 2, CH, BLK), b16),
            vm((SEG, NB + 2, CH, BLK), b16),
            vm((SEG, NB, CH, BLK), b16),
            vm((CH, BLK), b16),
            vm((CH, BLK), b16),
            vm((CH, BLK), b16),
            vm((CH, BLK), b16),
            vm((BLK, BLK), f32),
            vm((CH, BLK), f32),
            vm((SEG * 9 * GRP_CH, BLK), f32),
            vm((EXT, BLK), f32),
            vm((2 * CH, BLK), f32),
            vm((LAG, NB * 2 * CH, BLK), f32),
            vm((LAG, NB * 2 * CH, BLK), f32),
            vm((LAG, NB * EXT, BLK), f32),
            vm((LAG, NB * EXT, BLK), f32),
            vm((pairs, BLK), f32),
            vm((pairs, BLK), f32),
            vm((pairs, BLK), f32),
            vm((pairs, NLAG), f32),
            vm((pairs, NLAG), f32),
            vm((pairs, NLAG), b16),
            vm((pairs, NLAG), b16),
            vm((STAGES, PEERS, NOFF, NLAG), f32),
            pltpu.SemaphoreType.DMA((4, SEG + 1)),
            pltpu.SemaphoreType.DMA((4, SEG + 1)),
            pltpu.SemaphoreType.DMA((2, STAGES, PEERS)),
            pltpu.SemaphoreType.DMA((CH // GRP_CH + 5,)),
        ],
        compiler_params=pltpu.CompilerParams(
            collective_id=0, has_side_effects=True, vmem_limit_bytes=60 << 20
        ),
        name="whiten_correlate",
    )(ser, taps, keep_rows, offsets, *dft_tables())
    corr, stack = pl.pallas_call(
        hand_over,
        out_shape=(
            jax.ShapeDtypeStruct((pairs, NLAG), f32),
            jax.ShapeDtypeStruct((NOFF, NLAG), f32),
        ),
        in_specs=[hbm, hbm],
        out_specs=(hbm, hbm),
        scratch_shapes=[
            vm((pairs, NLAG), f32),
            vm((NOFF, NLAG), f32),
            pltpu.SemaphoreType.DMA((2, PIECES + 1)),
        ],
        compiler_params=pltpu.CompilerParams(vmem_limit_bytes=60 << 20),
        name="hand_over",
    )(corr, stack)
    return corr.reshape(CH, NOFF, NLAG), stack


def solution(mesh):
    spec3 = P(("grp", "dev"), None, None)
    spec2 = P(("grp", "dev"), None)
    shape = (mesh.shape["grp"], mesh.shape["dev"])
    return jax.shard_map(
        functools.partial(local, shape),
        mesh=mesh,
        in_specs=(spec3, spec2, spec2, P()),
        out_specs=(spec3, P()),
        check_vma=False,
    )
```

```python
import functools
import math

import jax
import jax.numpy as jnp
import numpy as np
from jax import lax
from jax.experimental import pallas as pl
from jax.experimental.pallas import tpu as pltpu
from jax.sharding import PartitionSpec as P

SEG = 6
SAMP = 1024
BLK = 128
TAPS = 64
NLAG = 128
NOFF = 8
CH = 64
NB = SAMP // BLK
NEAR = 3 * CH
EXT = 5 * CH
GRP_CH = 16
ROWS = NB * CH
QUART = 4
STAGES = 2
EARLY = 3
LAG = 3
PIECES = 4
PEERS = 16
FAR = (
    sorted(range(1, 16), key=lambda k: -min(k // 2, 8 - k // 2)),
    sorted(range(1, 16), key=lambda k: -(min(k // 4, 4 - k // 4) + (k // 2) % 2 * 2 + k % 2)),
)
MESH = pl.DeviceIdType.MESH


def split(t):
    t32 = t.astype(np.float32)
    hi = t32.astype(jnp.bfloat16)
    lo = (t32 - hi.astype(np.float32)).astype(jnp.bfloat16)
    return hi, lo


def dft_tables():
    n = np.arange(2 * BLK, dtype=np.float64)[:, None]
    f = np.arange(BLK, dtype=np.float64)[None, :] + 0.5
    ang = 2.0 * np.pi * f * n / (2 * BLK)
    full = np.concatenate([np.cos(ang), -np.sin(ang)], axis=1)
    half = BLK // 2
    own = full[:BLK]
    win = np.concatenate([full[half : half + BLK], full[half + BLK :], full[:half]], axis=0)
    m = np.arange(NLAG, dtype=np.float64)[None, :]
    ang_inv = 2.0 * np.pi * f.T * m / (2 * BLK)
    inv_hi, inv_lo = split(np.concatenate([np.cos(ang_inv), -np.sin(ang_inv)], axis=0) / BLK)
    inv = np.concatenate(
        [
            np.concatenate([inv_hi, inv_lo], axis=1),
            np.concatenate([inv_hi, np.zeros_like(inv_lo)], axis=1),
        ],
        axis=0,
    )
    return np.concatenate(split(own), axis=0), np.concatenate(split(win), axis=0), inv


def kernel(
    shape,
    ser_hbm,
    taps_hbm,
    keep_hbm,
    offs,
    own_hbm,
    win_hbm,
    inv_hbm,
    out_hbm,
    stack,
    ser,
    taps_in,
    keep_in,
    t_own,
    t_win,
    t_inv,
    white,
    p1,
    p2,
    m2,
    kv,
    k1,
    k2,
    km2,
    kt,
    tk,
    scr,
    keep_near,
    keep_left,
    xr,
    xi,
    yr,
    yi,
    accr,
    acci,
    scale,
    out,
    res,
    res_send,
    res_recv,
    got,
    ssem,
    rsem,
    qsem,
    lsem,
):
    ng, nd = shape
    f32, b16 = jnp.float32, jnp.bfloat16
    me_g, me_d = lax.axis_index("grp"), lax.axis_index("dev")

    def dev(k):
        t = lax.rem(me_g * nd + me_d + (k + ng * nd), ng * nd)
        return (t // nd, lax.rem(t, nd))

    core, my_y = lax.rem(me_g, 2), lax.rem(me_g // 2, 4)
    x_hi, x_lo = me_g // 8, me_d // 8
    z = lax.rem(me_d, 8)

    def peer(stage, k):
        c, yy, xh, xl, zz = core, my_y, x_hi, x_lo, z
        if stage == 1:
            yy = lax.rem(my_y + k // 4, 4)
            xh, xl = lax.rem(x_hi + k // 2 % 2, 2), lax.rem(x_lo + k % 2, 2)
        else:
            zz, c = lax.rem(z + k // 2, 8), lax.rem(core + k % 2, 2)
        return ((xh * 4 + yy) * 2 + c, xl * 8 + zz)

    bar = pltpu.get_barrier_semaphore()
    for k in (-2, -1, 1, 2):
        pl.semaphore_signal(bar, inc=1, device_id=dev(k), device_id_type=MESH)

    groups = CH // GRP_CH
    small = [
        pltpu.make_async_copy(taps_hbm, taps_in, lsem.at[groups]),
        pltpu.make_async_copy(keep_hbm, keep_in, lsem.at[groups + 1]),
    ]
    loads = [
        pltpu.make_async_copy(
            ser_hbm.at[:, pl.ds(g * GRP_CH, GRP_CH), :],
            ser.at[:, pl.ds(g * GRP_CH, GRP_CH), :],
            lsem.at[g],
        )
        for g in range(groups)
    ]
    tables = [
        pltpu.make_async_copy(src, dst, lsem.at[groups + 2 + i])
        for i, (src, dst) in enumerate(((own_hbm, t_own), (win_hbm, t_win), (inv_hbm, t_inv)))
    ]
    for copy in small + loads + tables:
        copy.start()

    for stage in range(STAGES):
        for k in range(1, PEERS):
            pl.semaphore_signal(bar, inc=1, device_id=peer(stage, k), device_id_type=MESH)

    kt[...] = jnp.zeros_like(kt)
    tk[...] = jnp.zeros_like(tk)
    for s in range(SEG):
        scr[pl.ds(s * 9 * GRP_CH, GRP_CH), :] = jnp.zeros((GRP_CH, BLK), f32)
    for copy in small:
        copy.wait()
    tk[:, pl.ds(0, TAPS)] = taps_in[...].astype(f32)
    kt[pl.ds(0, SEG), pl.ds(0, CH)] = keep_in[...].astype(f32)
    flags = jnp.transpose(kt[...])[:CH]
    keep_left[pl.ds(0, CH), :] = flags
    kv[...] = flags.astype(b16)

    def remote(src, dst, line, at, to):
        return pltpu.make_async_remote_copy(
            src_ref=src,
            dst_ref=dst,
            send_sem=ssem.at[line, at],
            recv_sem=rsem.at[line, at],
            device_id=dev(to),
            device_id_type=MESH,
        )

    def keep_copy(line):
        if line == 0:
            return remote(kv, k1, 0, SEG, -1)
        if line == 1:
            return remote(k1, k2, 1, SEG, -1)
        return remote(kv, km2, 2, SEG, 2)

    def seg_copy(line, s, first=0, count=CH):
        blocks, rows = pl.ds(1, NB), pl.ds(first, count)
        if line == 0:
            return remote(white.at[s, blocks, rows], p1.at[s, blocks, rows], 0, s, -1)
        if line == 1:
            return remote(p1.at[s, blocks, rows], p2.at[s, blocks, rows], 1, s, -1)
        return remote(white.at[s, blocks, rows], m2.at[s, :, rows], 2, s, 2)

    row_i = lax.broadcasted_iota(jnp.int32, (BLK, BLK), 0)
    col_i = lax.broadcasted_iota(jnp.int32, (BLK, BLK), 1)
    causal = col_i >= row_i
    row_lane = lax.broadcasted_iota(jnp.int32, (1, BLK), 1)

    for g in range(groups):
        loads[g].wait()
        for s in range(SEG):
            for b in range(NB):
                x = ser[s, pl.ds(g * GRP_CH, GRP_CH), pl.ds(b * BLK, BLK)]
                scr[pl.ds((s * 9 + b + 1) * GRP_CH, GRP_CH), :] = x.astype(f32)

        @pl.loop(0, GRP_CH, unroll=2)
        def _(c):
            cur = [scr[pl.ds((s * 9 + 1) * GRP_CH + c, NB, stride=GRP_CH), :] for s in range(SEG)]
            prv = [scr[pl.ds(s * 9 * GRP_CH + c, NB, stride=GRP_CH), :] for s in range(SEG)]
            x = jnp.concatenate(
                [jnp.concatenate(prv, axis=0), jnp.concatenate(cur, axis=0)], axis=1
            ).astype(b16)
            row = tk[pl.ds(g * GRP_CH + c, 1), :]
            circ = pltpu.roll(jnp.broadcast_to(row, (BLK, BLK)), 0, 1, stride=1, stride_axis=0)
            toep = jnp.concatenate(
                [jnp.where(causal, 0.0, circ), jnp.where(causal, circ, 0.0)], axis=0
            ).astype(b16)
            y = jnp.dot(x, toep, preferred_element_type=f32)
            for s in range(SEG):
                scr[pl.ds((s * 9 + 1) * GRP_CH + c, NB, stride=GRP_CH), :] = y[s * NB : (s + 1) * NB]

        mine = keep_left[pl.ds(g * GRP_CH, GRP_CH), :]
        for s in range(SEG):
            flag = jnp.broadcast_to(mine[:, s : s + 1], (GRP_CH, BLK))
            for b in range(NB):
                y = scr[pl.ds((s * 9 + b + 1) * GRP_CH, GRP_CH), :] * flag
                white[s, b + 1, pl.ds(g * GRP_CH, GRP_CH), :] = y.astype(b16)
        if g == 0:
            pl.semaphore_wait(bar, 4 + STAGES * (PEERS - 1))
            keep_copy(0).start()
            keep_copy(2).start()
        for s in range(EARLY):
            seg_copy(0, s, g * GRP_CH, GRP_CH).start()
            seg_copy(2, s, g * GRP_CH, GRP_CH).start()

    for s in range(EARLY, SEG):
        seg_copy(2, s).start()
    keep_copy(0).wait_recv()
    keep_copy(1).start()

    for s in range(SEG):
        for ref in (white, p1, p2):
            ref[s, 0] = jnp.zeros((CH, BLK), b16)
            ref[s, NB + 1] = jnp.zeros((CH, BLK), b16)
    accr[...] = jnp.zeros_like(accr)
    acci[...] = jnp.zeros_like(acci)

    def window_dft(src, s, turn, bases):
        nxt = jnp.where(row_lane < BLK // 2, 1.0, 0.0).astype(b16)
        prv = jnp.where(row_lane < BLK // 2, 0.0, 1.0).astype(b16)
        cur = src[s, pl.ds(1, NB)].reshape(ROWS, BLK)
        mix = src[s, pl.ds(2, NB)].reshape(ROWS, BLK) * nxt + src[s, pl.ds(0, NB)].reshape(ROWS, BLK) * prv
        x = jnp.concatenate([cur, mix, cur, mix], axis=1)
        y = jnp.dot(x, t_win[...], preferred_element_type=f32)
        for b in range(NB):
            for base in bases:
                yr[turn, pl.ds(b * EXT + base, CH), :] = y[b * CH : (b + 1) * CH, :BLK]
                yi[turn, pl.ds(b * EXT + base, CH), :] = y[b * CH : (b + 1) * CH, BLK:]

    def own_dft(src, s, turn, start, base):
        w = src[s, pl.ds(start, NB)].reshape(ROWS, BLK)
        y = jnp.dot(jnp.concatenate([w, w], axis=1), t_own[...], preferred_element_type=f32)
        for b in range(NB):
            xr[turn, pl.ds(b * 2 * CH + base, CH), :] = y[b * CH : (b + 1) * CH, :BLK]
            xi[turn, pl.ds(b * 2 * CH + base, CH), :] = y[b * CH : (b + 1) * CH, BLK:]

    eight = lax.broadcasted_iota(jnp.int32, (8, BLK), 0)
    per = CH // QUART

    def away(j, r0):
        return eight + (r0 + offs[j]) >= NEAR

    def slot(g, j):
        first = (g // (per // 8)) * (per * NOFF) + lax.rem(g, per // 8) * 8
        return pl.ds(pl.multiple_of(first + j * per, 8), 8)

    def pair_sums(turn, g):
        r0 = pl.multiple_of(g * 8, 8)
        far = [away(j, r0) for j in range(NOFF)]
        tr = [accr[slot(g, j), :] for j in range(NOFF)]
        ti = [acci[slot(g, j), :] for j in range(NOFF)]
        for b in range(NB):
            ar = xr[turn, pl.ds(b * 2 * CH + r0, 8), :]
            ai = xi[turn, pl.ds(b * 2 * CH + r0, 8), :]
            cr = xr[turn, pl.ds(b * 2 * CH + CH + r0, 8), :]
            ci = xi[turn, pl.ds(b * 2 * CH + CH + r0, 8), :]
            for j in range(NOFF):
                near = pl.ds(b * EXT + r0 + offs[j], 8)
                br = yr[turn, near, :]
                bi = yi[turn, near, :]
                lr = jnp.where(far[j], cr, ar)
                li = jnp.where(far[j], ci, ai)
                tr[j] = tr[j] + (lr * br + li * bi)
                ti[j] = ti[j] + (lr * bi - li * br)
        return tr, ti

    def first_dfts(s, turn):
        own_dft(white, s, turn, 1, 0)
        window_dft(white, s, turn, (0,))
        window_dft(p1, s, turn, (CH, 3 * CH))

    for copy in tables:
        copy.wait()

    def last_dfts(s, turn):
        seg_copy(2, s).wait_recv()
        own_dft(m2, s, turn, 0, CH)
        seg_copy(1, s).wait_recv()
        window_dft(p2, s, turn, (2 * CH, 4 * CH))

    @pl.loop(0, SEG - 1 + LAG)
    def _(step):
        @pl.when(step < SEG)
        def _():
            seg_copy(0, step).wait_recv()
            seg_copy(1, step).start()

        @pl.when(step < SEG - EARLY)
        def _():
            seg_copy(0, step + EARLY).start()

        @pl.when(step >= LAG)
        def _():
            turn = lax.rem(step - LAG, LAG)
            last_dfts(step - LAG, turn)

            @pl.loop(0, CH // 8)
            def _(g):
                tr, ti = pair_sums(turn, g)
                for j in range(NOFF):
                    accr[slot(g, j), :] = tr[j]
                    acci[slot(g, j), :] = ti[j]

        @pl.when(step < SEG)
        def _():
            first_dfts(step, lax.rem(step, LAG))

    keep_copy(1).wait_recv()
    keep_copy(2).wait_recv()
    keep_left[pl.ds(CH, CH), :] = km2[...].astype(f32)
    keep_near[pl.ds(0, CH), :] = kv[...].astype(f32)
    for base in (CH, 3 * CH):
        keep_near[pl.ds(base, CH), :] = k1[...].astype(f32)
    for base in (2 * CH, 4 * CH):
        keep_near[pl.ds(base, CH), :] = k2[...].astype(f32)

    @pl.loop(0, CH // 8)
    def _(g):
        r0 = pl.multiple_of(g * 8, 8)
        a = keep_left[pl.ds(r0, 8), :]
        c = keep_left[pl.ds(CH + r0, 8), :]
        for j in range(NOFF):
            near = keep_near[pl.ds(r0 + offs[j], 8), :]
            scale[slot(g, j), :] = jnp.where(away(j, r0), c, a) * near

    ones = jnp.ones((BLK, BLK), b16)
    number = jnp.dot(scale[...].astype(b16), ones, preferred_element_type=f32)
    scale[...] = 1.0 / (jnp.maximum(number, 1.0) * math.sqrt(SAMP))

    def back_copy(q):
        rows = pl.ds(q * per * NOFF, per * NOFF)
        return remote(res_send.at[rows], res_recv.at[rows], 3, q, -2)

    def out_copy(q):
        rows = pl.ds(q * per * NOFF, per * NOFF)
        return pltpu.make_async_copy(out.at[rows], out_hbm.at[rows], lsem.at[q])

    def lags(re, im):
        spec = jnp.concatenate([re, im], axis=1)
        hi = spec.astype(b16)
        lo = (spec - hi.astype(f32)).astype(b16)
        y = jnp.dot(jnp.concatenate([hi, lo], axis=1), t_inv[...], preferred_element_type=f32)
        return y[:, :NLAG] + y[:, NLAG:]

    def sum_copy(stage, k):
        return pltpu.make_async_remote_copy(
            src_ref=got.at[stage, 0],
            dst_ref=got.at[stage, k],
            send_sem=qsem.at[0, stage, k],
            recv_sem=qsem.at[1, stage, k],
            device_id=peer(stage, k),
            device_id_type=MESH,
        )

    def sum_start(stage):
        for k in FAR[stage]:
            sum_copy(stage, k).start()

    def sum_wait(stage):
        for k in range(1, PEERS):
            sum_copy(stage, k).wait_recv()
        return jnp.sum(got[stage], axis=0)

    turn = (SEG - 1) % LAG
    last_dfts(SEG - 1, turn)

    def finish(g, sums):
        tr, ti = pair_sums(turn, g)
        new = []
        for j in range(NOFF):
            by = scale[slot(g, j), :]
            tr[j] = tr[j] * by
            ti[j] = ti[j] * by
            accr[slot(g, j), :] = tr[j]
            acci[slot(g, j), :] = ti[j]
        return [t + u for t, u in zip(sums, tr + ti)]

    zero = jnp.zeros((8, BLK), f32)
    sums = lax.fori_loop(0, CH // 8, finish, [zero] * (2 * NOFF))
    sums = [jnp.sum(t, axis=0, keepdims=True) for t in sums]
    part = lags(jnp.concatenate(sums[:NOFF], axis=0), jnp.concatenate(sums[NOFF:], axis=0))
    got[0, 0] = part
    sum_start(0)

    for q in range(QUART):
        at = pl.ds(q * per * NOFF, per * NOFF)
        corr = lags(accr[at, :], acci[at, :])
        res[at, :] = corr
        res_send[at, :] = corr.astype(b16)
        back_copy(q).start()

    for stage in range(1, STAGES):
        got[stage, 0] = sum_wait(stage - 1)
        sum_start(stage)

    for q in range(QUART):
        back_copy(q).wait_recv()
        for j in range(NOFF):
            at = pl.ds((q * NOFF + j) * per, per)
            mine = res[at, :]
            theirs = res_recv[at, :].astype(f32)
            for h in range(per // 8):
                r0 = q * per + h * 8
                val = jnp.where(away(j, r0), theirs[h * 8 : h * 8 + 8], mine[h * 8 : h * 8 + 8])
                out[pl.ds(r0 * NOFF + j, 8, stride=NOFF), :] = val
        out_copy(q).start()

    for stage in range(STAGES):
        for k in range(1, PEERS):
            sum_copy(stage, k).wait_send()
    for q in range(QUART):
        out_copy(q).wait()
        back_copy(q).wait_send()

    @pl.loop(0, SEG)
    def _(s):
        for line in range(3):
            seg_copy(line, s).wait_send()

    for line in range(3):
        keep_copy(line).wait_send()
    stack[...] = sum_wait(STAGES - 1) * (1.0 / math.sqrt(CH * nd * ng))


def hand_over(corr_in, stack_in, corr, stack, held, small, sem):
    rows = CH * NOFF // PIECES
    parts = [pl.ds(i * rows, rows) for i in range(PIECES)]
    inward = [
        pltpu.make_async_copy(corr_in.at[p], held.at[p], sem.at[0, i]) for i, p in enumerate(parts)
    ]
    inward.append(pltpu.make_async_copy(stack_in, small, sem.at[0, PIECES]))
    outward = [
        pltpu.make_async_copy(held.at[p], corr.at[p], sem.at[1, i]) for i, p in enumerate(parts)
    ]
    outward.append(pltpu.make_async_copy(small, stack, sem.at[1, PIECES]))
    for copy in inward:
        copy.start()
    for arrived, leaving in zip(inward, outward):
        arrived.wait()
        leaving.start()
    for copy in outward:
        copy.wait()


def local(shape, series, taps, keep, offsets):
    ng, nd = shape
    f32, b16 = jnp.float32, jnp.bfloat16
    ser = jnp.transpose(series, (1, 0, 2))
    keep_rows = jnp.transpose(keep, (1, 0))
    vmem = pl.BlockSpec(memory_space=pltpu.VMEM)
    smem = pl.BlockSpec(memory_space=pltpu.SMEM)
    hbm = pl.BlockSpec(memory_space=pltpu.HBM)
    pairs = CH * NOFF
    vm = pltpu.VMEM
    corr, stack = pl.pallas_call(
        functools.partial(kernel, shape),
        out_shape=(
            jax.ShapeDtypeStruct((pairs, NLAG), f32),
            jax.ShapeDtypeStruct((NOFF, NLAG), f32),
        ),
        in_specs=[hbm, hbm, hbm, smem, hbm, hbm, hbm],
        out_specs=(hbm, vmem),
        scratch_shapes=[
            vm((SEG, CH, SAMP), b16),
            vm((CH, TAPS), b16),
            vm((SEG, CH), jnp.int32),
            vm((2 * BLK, 2 * BLK), b16),
            vm((4 * BLK, 2 * BLK), b16),
            vm((4 * BLK, 2 * NLAG), b16),
            vm((SEG, NB + 2, CH, BLK), b16),
            vm((SEG, NB + 2, CH, BLK), b16),
            vm((SEG, NB + 2, CH, BLK), b16),
            vm((SEG, NB, CH, BLK), b16),
            vm((CH, BLK), b16),
            vm((CH, BLK), b16),
            vm((CH, BLK), b16),
            vm((CH, BLK), b16),
            vm((BLK, BLK), f32),
            vm((CH, BLK), f32),
            vm((SEG * 9 * GRP_CH, BLK), f32),
            vm((EXT, BLK), f32),
            vm((2 * CH, BLK), f32),
            vm((LAG, NB * 2 * CH, BLK), f32),
            vm((LAG, NB * 2 * CH, BLK), f32),
            vm((LAG, NB * EXT, BLK), f32),
            vm((LAG, NB * EXT, BLK), f32),
            vm((pairs, BLK), f32),
            vm((pairs, BLK), f32),
            vm((pairs, BLK), f32),
            vm((pairs, NLAG), f32),
            vm((pairs, NLAG), f32),
            vm((pairs, NLAG), b16),
            vm((pairs, NLAG), b16),
            vm((STAGES, PEERS, NOFF, NLAG), f32),
            pltpu.SemaphoreType.DMA((4, SEG + 1)),
            pltpu.SemaphoreType.DMA((4, SEG + 1)),
            pltpu.SemaphoreType.DMA((2, STAGES, PEERS)),
            pltpu.SemaphoreType.DMA((CH // GRP_CH + 5,)),
        ],
        compiler_params=pltpu.CompilerParams(
            collective_id=0, has_side_effects=True, vmem_limit_bytes=60 << 20
        ),
        name="whiten_correlate",
    )(ser, taps, keep_rows, offsets, *dft_tables())
    corr, stack = pl.pallas_call(
        hand_over,
        out_shape=(
            jax.ShapeDtypeStruct((pairs, NLAG), f32),
            jax.ShapeDtypeStruct((NOFF, NLAG), f32),
        ),
        in_specs=[hbm, hbm],
        out_specs=(hbm, hbm),
        scratch_shapes=[
            vm((pairs, NLAG), f32),
            vm((NOFF, NLAG), f32),
            pltpu.SemaphoreType.DMA((2, PIECES + 1)),
        ],
        compiler_params=pltpu.CompilerParams(vmem_limit_bytes=60 << 20),
        name="hand_over",
    )(corr, stack)
    return corr.reshape(CH, NOFF, NLAG), stack


def solution(mesh):
    spec3 = P(("grp", "dev"), None, None)
    spec2 = P(("grp", "dev"), None)
    shape = (mesh.shape["grp"], mesh.shape["dev"])
    return jax.shard_map(
        functools.partial(local, shape),
        mesh=mesh,
        in_specs=(spec3, spec2, spec2, P()),
        out_specs=(spec3, P()),
        check_vma=False,
    )
```

```python
import functools
import math

import jax
import jax.numpy as jnp
import numpy as np
from jax import lax
from jax.experimental import pallas as pl
from jax.experimental.pallas import tpu as pltpu
from jax.sharding import PartitionSpec as P

SEG = 6
SAMP = 1024
BLK = 128
TAPS = 64
NLAG = 128
NOFF = 8
CH = 64
NB = SAMP // BLK
NEAR = 3 * CH
EXT = 5 * CH
GRP_CH = 16
ROWS = NB * CH
QUART = 4
STAGES = 2
EARLY = 3
LAG = 3
PIECES = 4
PEERS = 16
FAR = (
    sorted(range(1, 16), key=lambda k: -min(k // 2, 8 - k // 2)),
    sorted(range(1, 16), key=lambda k: -(min(k // 4, 4 - k // 4) + (k // 2) % 2 * 2 + k % 2)),
)
MESH = pl.DeviceIdType.MESH


def split(t):
    t32 = t.astype(np.float32)
    hi = t32.astype(jnp.bfloat16)
    lo = (t32 - hi.astype(np.float32)).astype(jnp.bfloat16)
    return hi, lo


def dft_tables():
    n = np.arange(2 * BLK, dtype=np.float64)[:, None]
    f = np.arange(BLK, dtype=np.float64)[None, :] + 0.5
    ang = 2.0 * np.pi * f * n / (2 * BLK)
    full = np.concatenate([np.cos(ang), -np.sin(ang)], axis=1)
    half = BLK // 2
    own = full[:BLK]
    win = np.concatenate([full[half : half + BLK], full[half + BLK :], full[:half]], axis=0)
    m = np.arange(NLAG, dtype=np.float64)[None, :]
    ang_inv = 2.0 * np.pi * f.T * m / (2 * BLK)
    inv_hi, inv_lo = split(np.concatenate([np.cos(ang_inv), -np.sin(ang_inv)], axis=0) / BLK)
    inv = np.concatenate(
        [
            np.concatenate([inv_hi, inv_lo], axis=1),
            np.concatenate([inv_hi, np.zeros_like(inv_lo)], axis=1),
        ],
        axis=0,
    )
    return np.concatenate(split(own), axis=0), np.concatenate(split(win), axis=0), inv


def kernel(
    shape,
    ser_hbm,
    taps_hbm,
    keep_hbm,
    offs,
    own_hbm,
    win_hbm,
    inv_hbm,
    out_hbm,
    stack,
    ser,
    taps_in,
    keep_in,
    t_own,
    t_win,
    t_inv,
    white,
    p1,
    p2,
    m2,
    kv,
    k1,
    k2,
    km2,
    kt,
    tk,
    scr,
    keep_near,
    keep_left,
    xr,
    xi,
    yr,
    yi,
    accr,
    acci,
    scale,
    out,
    res,
    res_send,
    res_recv,
    got,
    ssem,
    rsem,
    qsem,
    lsem,
):
    ng, nd = shape
    f32, b16 = jnp.float32, jnp.bfloat16
    me_g, me_d = lax.axis_index("grp"), lax.axis_index("dev")

    def dev(k):
        t = lax.rem(me_g * nd + me_d + (k + ng * nd), ng * nd)
        return (t // nd, lax.rem(t, nd))

    core, my_y = lax.rem(me_g, 2), lax.rem(me_g // 2, 4)
    x_hi, x_lo = me_g // 8, me_d // 8
    z = lax.rem(me_d, 8)

    def peer(stage, k):
        c, yy, xh, xl, zz = core, my_y, x_hi, x_lo, z
        if stage == 1:
            yy = lax.rem(my_y + k // 4, 4)
            xh, xl = lax.rem(x_hi + k // 2 % 2, 2), lax.rem(x_lo + k % 2, 2)
        else:
            zz, c = lax.rem(z + k // 2, 8), lax.rem(core + k % 2, 2)
        return ((xh * 4 + yy) * 2 + c, xl * 8 + zz)

    groups = CH // GRP_CH
    small = [
        pltpu.make_async_copy(taps_hbm, taps_in, lsem.at[groups]),
        pltpu.make_async_copy(keep_hbm, keep_in, lsem.at[groups + 1]),
    ]
    loads = [
        pltpu.make_async_copy(
            ser_hbm.at[:, pl.ds(g * GRP_CH, GRP_CH), :],
            ser.at[:, pl.ds(g * GRP_CH, GRP_CH), :],
            lsem.at[g],
        )
        for g in range(groups)
    ]
    tables = [
        pltpu.make_async_copy(src, dst, lsem.at[groups + 2 + i])
        for i, (src, dst) in enumerate(((own_hbm, t_own), (win_hbm, t_win), (inv_hbm, t_inv)))
    ]
    for copy in small + loads + tables:
        copy.start()

    bar = pltpu.get_barrier_semaphore()
    for k in (-2, -1, 1, 2):
        pl.semaphore_signal(bar, inc=1, device_id=dev(k), device_id_type=MESH)

    for stage in range(STAGES):
        for k in range(1, PEERS):
            pl.semaphore_signal(bar, inc=1, device_id=peer(stage, k), device_id_type=MESH)

    kt[...] = jnp.zeros_like(kt)
    tk[...] = jnp.zeros_like(tk)
    for s in range(SEG):
        scr[pl.ds(s * 9 * GRP_CH, GRP_CH), :] = jnp.zeros((GRP_CH, BLK), f32)
    for copy in small:
        copy.wait()
    tk[:, pl.ds(0, TAPS)] = taps_in[...].astype(f32)
    kt[pl.ds(0, SEG), pl.ds(0, CH)] = keep_in[...].astype(f32)
    flags = jnp.transpose(kt[...])[:CH]
    keep_left[pl.ds(0, CH), :] = flags
    kv[...] = flags.astype(b16)

    def remote(src, dst, line, at, to):
        return pltpu.make_async_remote_copy(
            src_ref=src,
            dst_ref=dst,
            send_sem=ssem.at[line, at],
            recv_sem=rsem.at[line, at],
            device_id=dev(to),
            device_id_type=MESH,
        )

    def keep_copy(line):
        if line == 0:
            return remote(kv, k1, 0, SEG, -1)
        if line == 1:
            return remote(k1, k2, 1, SEG, -1)
        return remote(kv, km2, 2, SEG, 2)

    def seg_copy(line, s, first=0, count=CH):
        blocks, rows = pl.ds(1, NB), pl.ds(first, count)
        if line == 0:
            return remote(white.at[s, blocks, rows], p1.at[s, blocks, rows], 0, s, -1)
        if line == 1:
            return remote(p1.at[s, blocks, rows], p2.at[s, blocks, rows], 1, s, -1)
        return remote(white.at[s, blocks, rows], m2.at[s, :, rows], 2, s, 2)

    row_i = lax.broadcasted_iota(jnp.int32, (BLK, BLK), 0)
    col_i = lax.broadcasted_iota(jnp.int32, (BLK, BLK), 1)
    causal = col_i >= row_i
    row_lane = lax.broadcasted_iota(jnp.int32, (1, BLK), 1)

    for g in range(groups):
        loads[g].wait()
        for s in range(SEG):
            for b in range(NB):
                x = ser[s, pl.ds(g * GRP_CH, GRP_CH), pl.ds(b * BLK, BLK)]
                scr[pl.ds((s * 9 + b + 1) * GRP_CH, GRP_CH), :] = x.astype(f32)

        @pl.loop(0, GRP_CH, unroll=2)
        def _(c):
            cur = [scr[pl.ds((s * 9 + 1) * GRP_CH + c, NB, stride=GRP_CH), :] for s in range(SEG)]
            prv = [scr[pl.ds(s * 9 * GRP_CH + c, NB, stride=GRP_CH), :] for s in range(SEG)]
            x = jnp.concatenate(
                [jnp.concatenate(prv, axis=0), jnp.concatenate(cur, axis=0)], axis=1
            ).astype(b16)
            row = tk[pl.ds(g * GRP_CH + c, 1), :]
            circ = pltpu.roll(jnp.broadcast_to(row, (BLK, BLK)), 0, 1, stride=1, stride_axis=0)
            toep = jnp.concatenate(
                [jnp.where(causal, 0.0, circ), jnp.where(causal, circ, 0.0)], axis=0
            ).astype(b16)
            y = jnp.dot(x, toep, preferred_element_type=f32)
            for s in range(SEG):
                scr[pl.ds((s * 9 + 1) * GRP_CH + c, NB, stride=GRP_CH), :] = y[s * NB : (s + 1) * NB]

        mine = keep_left[pl.ds(g * GRP_CH, GRP_CH), :]
        for s in range(SEG):
            flag = jnp.broadcast_to(mine[:, s : s + 1], (GRP_CH, BLK))
            for b in range(NB):
                y = scr[pl.ds((s * 9 + b + 1) * GRP_CH, GRP_CH), :] * flag
                white[s, b + 1, pl.ds(g * GRP_CH, GRP_CH), :] = y.astype(b16)
        if g == 0:
            pl.semaphore_wait(bar, 4 + STAGES * (PEERS - 1))
            keep_copy(0).start()
            keep_copy(2).start()
        for s in range(EARLY):
            seg_copy(0, s, g * GRP_CH, GRP_CH).start()
            seg_copy(2, s, g * GRP_CH, GRP_CH).start()

    for s in range(EARLY, SEG):
        seg_copy(2, s).start()
    keep_copy(0).wait_recv()
    keep_copy(1).start()

    for s in range(SEG):
        for ref in (white, p1, p2):
            ref[s, 0] = jnp.zeros((CH, BLK), b16)
            ref[s, NB + 1] = jnp.zeros((CH, BLK), b16)
    accr[...] = jnp.zeros_like(accr)
    acci[...] = jnp.zeros_like(acci)

    def window_dft(src, s, turn, bases):
        nxt = jnp.where(row_lane < BLK // 2, 1.0, 0.0).astype(b16)
        prv = jnp.where(row_lane < BLK // 2, 0.0, 1.0).astype(b16)
        cur = src[s, pl.ds(1, NB)].reshape(ROWS, BLK)
        mix = src[s, pl.ds(2, NB)].reshape(ROWS, BLK) * nxt + src[s, pl.ds(0, NB)].reshape(ROWS, BLK) * prv
        x = jnp.concatenate([cur, mix, cur, mix], axis=1)
        y = jnp.dot(x, t_win[...], preferred_element_type=f32)
        for b in range(NB):
            for base in bases:
                yr[turn, pl.ds(b * EXT + base, CH), :] = y[b * CH : (b + 1) * CH, :BLK]
                yi[turn, pl.ds(b * EXT + base, CH), :] = y[b * CH : (b + 1) * CH, BLK:]

    def own_dft(src, s, turn, start, base):
        w = src[s, pl.ds(start, NB)].reshape(ROWS, BLK)
        y = jnp.dot(jnp.concatenate([w, w], axis=1), t_own[...], preferred_element_type=f32)
        for b in range(NB):
            xr[turn, pl.ds(b * 2 * CH + base, CH), :] = y[b * CH : (b + 1) * CH, :BLK]
            xi[turn, pl.ds(b * 2 * CH + base, CH), :] = y[b * CH : (b + 1) * CH, BLK:]

    eight = lax.broadcasted_iota(jnp.int32, (8, BLK), 0)
    per = CH // QUART

    def away(j, r0):
        return eight + (r0 + offs[j]) >= NEAR

    def slot(g, j):
        first = (g // (per // 8)) * (per * NOFF) + lax.rem(g, per // 8) * 8
        return pl.ds(pl.multiple_of(first + j * per, 8), 8)

    def pair_sums(turn, g):
        r0 = pl.multiple_of(g * 8, 8)
        far = [away(j, r0) for j in range(NOFF)]
        tr = [accr[slot(g, j), :] for j in range(NOFF)]
        ti = [acci[slot(g, j), :] for j in range(NOFF)]
        for b in range(NB):
            ar = xr[turn, pl.ds(b * 2 * CH + r0, 8), :]
            ai = xi[turn, pl.ds(b * 2 * CH + r0, 8), :]
            cr = xr[turn, pl.ds(b * 2 * CH + CH + r0, 8), :]
            ci = xi[turn, pl.ds(b * 2 * CH + CH + r0, 8), :]
            for j in range(NOFF):
                near = pl.ds(b * EXT + r0 + offs[j], 8)
                br = yr[turn, near, :]
                bi = yi[turn, near, :]
                lr = jnp.where(far[j], cr, ar)
                li = jnp.where(far[j], ci, ai)
                tr[j] = tr[j] + (lr * br + li * bi)
                ti[j] = ti[j] + (lr * bi - li * br)
        return tr, ti

    def first_dfts(s, turn):
        own_dft(white, s, turn, 1, 0)
        window_dft(white, s, turn, (0,))
        window_dft(p1, s, turn, (CH, 3 * CH))

    for copy in tables:
        copy.wait()

    def last_dfts(s, turn):
        seg_copy(2, s).wait_recv()
        own_dft(m2, s, turn, 0, CH)
        seg_copy(1, s).wait_recv()
        window_dft(p2, s, turn, (2 * CH, 4 * CH))

    @pl.loop(0, SEG - 1 + LAG)
    def _(step):
        @pl.when(step < SEG)
        def _():
            seg_copy(0, step).wait_recv()
            seg_copy(1, step).start()

        @pl.when(step < SEG - EARLY)
        def _():
            seg_copy(0, step + EARLY).start()

        @pl.when(step >= LAG)
        def _():
            turn = lax.rem(step - LAG, LAG)
            last_dfts(step - LAG, turn)

            @pl.loop(0, CH // 8)
            def _(g):
                tr, ti = pair_sums(turn, g)
                for j in range(NOFF):
                    accr[slot(g, j), :] = tr[j]
                    acci[slot(g, j), :] = ti[j]

        @pl.when(step < SEG)
        def _():
            first_dfts(step, lax.rem(step, LAG))

    keep_copy(1).wait_recv()
    keep_copy(2).wait_recv()
    keep_left[pl.ds(CH, CH), :] = km2[...].astype(f32)
    keep_near[pl.ds(0, CH), :] = kv[...].astype(f32)
    for base in (CH, 3 * CH):
        keep_near[pl.ds(base, CH), :] = k1[...].astype(f32)
    for base in (2 * CH, 4 * CH):
        keep_near[pl.ds(base, CH), :] = k2[...].astype(f32)

    @pl.loop(0, CH // 8)
    def _(g):
        r0 = pl.multiple_of(g * 8, 8)
        a = keep_left[pl.ds(r0, 8), :]
        c = keep_left[pl.ds(CH + r0, 8), :]
        for j in range(NOFF):
            near = keep_near[pl.ds(r0 + offs[j], 8), :]
            scale[slot(g, j), :] = jnp.where(away(j, r0), c, a) * near

    ones = jnp.ones((BLK, BLK), b16)
    number = jnp.dot(scale[...].astype(b16), ones, preferred_element_type=f32)
    scale[...] = 1.0 / (jnp.maximum(number, 1.0) * math.sqrt(SAMP))

    def back_copy(q):
        rows = pl.ds(q * per * NOFF, per * NOFF)
        return remote(res_send.at[rows], res_recv.at[rows], 3, q, -2)

    def out_copy(q):
        rows = pl.ds(q * per * NOFF, per * NOFF)
        return pltpu.make_async_copy(out.at[rows], out_hbm.at[rows], lsem.at[q])

    def lags(re, im):
        spec = jnp.concatenate([re, im], axis=1)
        hi = spec.astype(b16)
        lo = (spec - hi.astype(f32)).astype(b16)
        y = jnp.dot(jnp.concatenate([hi, lo], axis=1), t_inv[...], preferred_element_type=f32)
        return y[:, :NLAG] + y[:, NLAG:]

    def sum_copy(stage, k):
        return pltpu.make_async_remote_copy(
            src_ref=got.at[stage, 0],
            dst_ref=got.at[stage, k],
            send_sem=qsem.at[0, stage, k],
            recv_sem=qsem.at[1, stage, k],
            device_id=peer(stage, k),
            device_id_type=MESH,
        )

    def sum_start(stage):
        for k in FAR[stage]:
            sum_copy(stage, k).start()

    def sum_wait(stage):
        for k in range(1, PEERS):
            sum_copy(stage, k).wait_recv()
        return jnp.sum(got[stage], axis=0)

    turn = (SEG - 1) % LAG
    last_dfts(SEG - 1, turn)

    def finish(g, sums):
        tr, ti = pair_sums(turn, g)
        new = []
        for j in range(NOFF):
            by = scale[slot(g, j), :]
            tr[j] = tr[j] * by
            ti[j] = ti[j] * by
            accr[slot(g, j), :] = tr[j]
            acci[slot(g, j), :] = ti[j]
        return [t + u for t, u in zip(sums, tr + ti)]

    zero = jnp.zeros((8, BLK), f32)
    sums = lax.fori_loop(0, CH // 8, finish, [zero] * (2 * NOFF))
    sums = [jnp.sum(t, axis=0, keepdims=True) for t in sums]
    part = lags(jnp.concatenate(sums[:NOFF], axis=0), jnp.concatenate(sums[NOFF:], axis=0))
    got[0, 0] = part
    sum_start(0)

    for q in range(QUART):
        at = pl.ds(q * per * NOFF, per * NOFF)
        corr = lags(accr[at, :], acci[at, :])
        res[at, :] = corr
        res_send[at, :] = corr.astype(b16)
        back_copy(q).start()

    for stage in range(1, STAGES):
        got[stage, 0] = sum_wait(stage - 1)
        sum_start(stage)

    for q in range(QUART):
        back_copy(q).wait_recv()
        for j in range(NOFF):
            at = pl.ds((q * NOFF + j) * per, per)
            mine = res[at, :]
            theirs = res_recv[at, :].astype(f32)
            for h in range(per // 8):
                r0 = q * per + h * 8
                val = jnp.where(away(j, r0), theirs[h * 8 : h * 8 + 8], mine[h * 8 : h * 8 + 8])
                out[pl.ds(r0 * NOFF + j, 8, stride=NOFF), :] = val
        out_copy(q).start()

    for stage in range(STAGES):
        for k in range(1, PEERS):
            sum_copy(stage, k).wait_send()
    for q in range(QUART):
        out_copy(q).wait()
        back_copy(q).wait_send()

    @pl.loop(0, SEG)
    def _(s):
        for line in range(3):
            seg_copy(line, s).wait_send()

    for line in range(3):
        keep_copy(line).wait_send()
    stack[...] = sum_wait(STAGES - 1) * (1.0 / math.sqrt(CH * nd * ng))


def hand_over(corr_in, stack_in, corr, stack, held, small, sem):
    rows = CH * NOFF // PIECES
    parts = [pl.ds(i * rows, rows) for i in range(PIECES)]
    inward = [
        pltpu.make_async_copy(corr_in.at[p], held.at[p], sem.at[0, i]) for i, p in enumerate(parts)
    ]
    inward.append(pltpu.make_async_copy(stack_in, small, sem.at[0, PIECES]))
    outward = [
        pltpu.make_async_copy(held.at[p], corr.at[p], sem.at[1, i]) for i, p in enumerate(parts)
    ]
    outward.append(pltpu.make_async_copy(small, stack, sem.at[1, PIECES]))
    for copy in inward:
        copy.start()
    for arrived, leaving in zip(inward, outward):
        arrived.wait()
        leaving.start()
    for copy in outward:
        copy.wait()


def local(shape, series, taps, keep, offsets):
    ng, nd = shape
    f32, b16 = jnp.float32, jnp.bfloat16
    ser = jnp.transpose(series, (1, 0, 2))
    keep_rows = jnp.transpose(keep, (1, 0))
    vmem = pl.BlockSpec(memory_space=pltpu.VMEM)
    smem = pl.BlockSpec(memory_space=pltpu.SMEM)
    hbm = pl.BlockSpec(memory_space=pltpu.HBM)
    pairs = CH * NOFF
    vm = pltpu.VMEM
    corr, stack = pl.pallas_call(
        functools.partial(kernel, shape),
        out_shape=(
            jax.ShapeDtypeStruct((pairs, NLAG), f32),
            jax.ShapeDtypeStruct((NOFF, NLAG), f32),
        ),
        in_specs=[hbm, hbm, hbm, smem, hbm, hbm, hbm],
        out_specs=(hbm, vmem),
        scratch_shapes=[
            vm((SEG, CH, SAMP), b16),
            vm((CH, TAPS), b16),
            vm((SEG, CH), jnp.int32),
            vm((2 * BLK, 2 * BLK), b16),
            vm((4 * BLK, 2 * BLK), b16),
            vm((4 * BLK, 2 * NLAG), b16),
            vm((SEG, NB + 2, CH, BLK), b16),
            vm((SEG, NB + 2, CH, BLK), b16),
            vm((SEG, NB + 2, CH, BLK), b16),
            vm((SEG, NB, CH, BLK), b16),
            vm((CH, BLK), b16),
            vm((CH, BLK), b16),
            vm((CH, BLK), b16),
            vm((CH, BLK), b16),
            vm((BLK, BLK), f32),
            vm((CH, BLK), f32),
            vm((SEG * 9 * GRP_CH, BLK), f32),
            vm((EXT, BLK), f32),
            vm((2 * CH, BLK), f32),
            vm((LAG, NB * 2 * CH, BLK), f32),
            vm((LAG, NB * 2 * CH, BLK), f32),
            vm((LAG, NB * EXT, BLK), f32),
            vm((LAG, NB * EXT, BLK), f32),
            vm((pairs, BLK), f32),
            vm((pairs, BLK), f32),
            vm((pairs, BLK), f32),
            vm((pairs, NLAG), f32),
            vm((pairs, NLAG), f32),
            vm((pairs, NLAG), b16),
            vm((pairs, NLAG), b16),
            vm((STAGES, PEERS, NOFF, NLAG), f32),
            pltpu.SemaphoreType.DMA((4, SEG + 1)),
            pltpu.SemaphoreType.DMA((4, SEG + 1)),
            pltpu.SemaphoreType.DMA((2, STAGES, PEERS)),
            pltpu.SemaphoreType.DMA((CH // GRP_CH + 5,)),
        ],
        compiler_params=pltpu.CompilerParams(
            collective_id=0, has_side_effects=True, vmem_limit_bytes=60 << 20
        ),
        name="whiten_correlate",
    )(ser, taps, keep_rows, offsets, *dft_tables())
    corr, stack = pl.pallas_call(
        hand_over,
        out_shape=(
            jax.ShapeDtypeStruct((pairs, NLAG), f32),
            jax.ShapeDtypeStruct((NOFF, NLAG), f32),
        ),
        in_specs=[hbm, hbm],
        out_specs=(hbm, hbm),
        scratch_shapes=[
            vm((pairs, NLAG), f32),
            vm((NOFF, NLAG), f32),
            pltpu.SemaphoreType.DMA((2, PIECES + 1)),
        ],
        compiler_params=pltpu.CompilerParams(vmem_limit_bytes=60 << 20),
        name="hand_over",
    )(corr, stack)
    return corr.reshape(CH, NOFF, NLAG), stack


def solution(mesh):
    spec3 = P(("grp", "dev"), None, None)
    spec2 = P(("grp", "dev"), None)
    shape = (mesh.shape["grp"], mesh.shape["dev"])
    return jax.shard_map(
        functools.partial(local, shape),
        mesh=mesh,
        in_specs=(spec3, spec2, spec2, P()),
        out_specs=(spec3, P()),
        check_vma=False,
    )
```
